128 devices in a mesh: dp: 32 (over z, x, core), seq: 4 (over y).
Axes of the slice: x: 4, y: 4, z: 4, core: 2. Of those that a mesh axis runs over, the one named last changes fastest.
Arguments:
- tokens: bfloat16 [64, 1024, 768], P('dp', 'seq'), may hold values from -6 to 6
- buckets: int32 [64, 1024, 1], P('dp', 'seq'), may hold values from 0 to 63; in each aligned block of 256 rows (0 to 255, 256 to 511, ..., all dimensions but the last counted through in order) at most 8 rows name the same one
- qkv_weight: bfloat16 [768, 2304], P(('dp', 'seq')), may hold values from -0.21875 to 0.21875
- output_weight: bfloat16 [768, 768], P(('dp', 'seq')), may hold values from -1.75 to 1.75
- attend_gain: bfloat16 [768], P(('dp', 'seq')), may hold values from 0.5 to 1.5
- attend_bias: bfloat16 [768], P(('dp', 'seq')), may hold values from -1 to 1
- expert_gain: bfloat16 [768], P(('dp', 'seq')), may hold values from 0.5 to 1.5
- expert_bias: bfloat16 [768], P(('dp', 'seq')), may hold values from -1 to 1
- expert_in: bfloat16 [64, 768, 3072], P('dp', None, 'seq'), may hold values from -0.21875 to 0.21875
- expert_out: bfloat16 [64, 3072, 768], P('dp', 'seq'), may hold values from -0.15625 to 0.15625
- cotangent: bfloat16 [64, 1024, 768], P('dp', 'seq'), may hold values from -6 to 6
Outputs:
- block_out: bfloat16 [64, 1024, 768], P('dp', 'seq')
- token_grad: bfloat16 [64, 1024, 768], P('dp', 'seq')
- qkv_grad: float32 [768, 2304], P(('dp', 'seq'))
- outproj_grad: float32 [768, 768], P(('dp', 'seq'))
- attgain_grad: float32 [768], P(('dp', 'seq'))
- attbias_grad: float32 [768], P(('dp', 'seq'))
- expgain_grad: float32 [768], P(('dp', 'seq'))
- expbias_grad: float32 [768], P(('dp', 'seq'))
- expin_grad: float32 [64, 768, 3072], P('dp', None, 'seq')
- expout_grad: float32 [64, 3072, 768], P('dp', 'seq')
The draws below stay inside these ranges and needn't reach their ends.
Inputs may be any that keep to these rules, and one draw needn't show every extreme that they name: `buckets`: in each sequence's block of 256 tokens on one index of seq no bucket holds more than 8 tokens, and some bucket holds exactly 8 in some blocks of every draw.
All inputs are finite; a program needn't handle non-finite values.
Results may differ from the reference program's by a relative error of at most 0.015.
Values may be sent and summed in bfloat16 or wider, within the bound.
No kernel may reach another device: no remote copies, remote signals or barrier semaphores. Data moves between devices by JAX's collectives and lax.ppermute only.
A program may use at most 192 MiB of HBM per device.

```python
import math
from functools import partial
import jax
import jax.numpy as jnp
import numpy as np
from jax import lax

D = 768
HEADS = 12
HEAD_DIM = 64
FF = 3072
LENGTH = 1024
BATCH = 64
EXPERTS = 64
PART = 256
SLOT = 8
N_SEQ = 4


def block_scale(stream_key, dims, pieces, low, high):
    loudness = 1.0
    for position, shards_of in pieces:
        draws = jax.random.uniform(jax.random.fold_in(jax.random.fold_in(stream_key, 6), position), (shards_of,), jnp.float32, low / len(pieces), high / len(pieces))
        loudness = loudness * jnp.repeat(jnp.exp(draws), dims[position] // shards_of).reshape((-1,) + (1,) * (len(dims) - 1 - position))
    return loudness


def assign_block(stream_key, own, number, rows, count, top, most, lean):
    sequence = jax.random.permutation(stream_key, count)
    packed, common = load_shares(count, rows * top, most, lean, True), load_shares(count, rows * top, most, lean, False)
    places = jnp.arange(count)

    def named(tallies, rotation):
        used = int((tallies > 0).sum())
        fixed = max(1, used // 4)
        passed = fixed + (places - fixed + rotation * (used - fixed)) % max(1, count - fixed)
        return jnp.zeros((count,), jnp.int32).at[sequence[jnp.where(places < fixed, places, passed)]].set(jnp.asarray(tallies, jnp.int32))

    tallies = jnp.where(number % 4 == 0, named(packed, number // 4), named(common, number - number // 4 - 1))
    mixed = jax.random.permutation(jax.random.fold_in(own, 3), count)
    source_of, taker = mixed[0:count // 2 * 2:2], mixed[1:count // 2 * 2:2]
    margin = jnp.minimum(tallies[source_of] - 1, most - tallies[taker]) // 2
    margin = jnp.where((source_of == sequence[0]) | (taker == sequence[0]) | (tallies[taker] == 0), 0, jnp.maximum(margin, 0))
    passed = jax.random.randint(jax.random.fold_in(own, 4), (count // 2,), 0, 1 << 20) % (margin + 1)
    tallies = tallies.at[source_of].add(-passed).at[taker].add(passed)
    items = jnp.searchsorted(jnp.cumsum(tallies), jnp.arange(rows * top), side="right").astype(jnp.int32)
    grid = items.reshape(top, rows).T
    grid = grid[jax.random.permutation(jax.random.fold_in(own, 1), rows)]
    rotation = jax.random.randint(jax.random.fold_in(own, 2), (rows, 1), 0, top)
    return jnp.take_along_axis(grid, (jnp.arange(top)[None, :] + rotation) % top, axis=1)


def load_shares(number_of, total, reach, slope, full):
    weights = [(1 << 20) // math.isqrt(standing ** slope) + 1 for standing in range(1, number_of + 1)]
    largest = reach if full else min(reach, max(-(-total // number_of), total * weights[0] // sum(weights)))
    least = 1 if total - largest >= number_of - 1 else 0
    holding, rest = [largest] + [least] * (number_of - 1), total - largest - least * (number_of - 1)
    while rest > 0:
        free = [i for i in range(1, number_of) if holding[i] < largest] or [i for i in range(1, number_of) if holding[i] < reach]
        pool, budget = sum([weights[i] for i in free]), rest
        for i in free:
            more = min(reach - holding[i], max(1, budget * weights[i] // pool), rest)
            holding[i] = holding[i] + more
            rest = rest - more
    return np.array(holding)


def scatter_about(rng, extent, spread, bound, pieces=(), held_as=jnp.bfloat16):
    level = block_scale(rng, extent, pieces, -0.22, 0.18) if pieces else 1.0
    array = jax.random.normal(rng, extent, jnp.float32) * spread * level
    return jnp.minimum(jnp.maximum(array, -bound), bound).astype(held_as)


def setup_inputs(seed: int = 0) -> dict:
    splits = jax.random.split(jax.random.key(seed), 12)
    tokens = scatter_about(splits[0], (BATCH, LENGTH, D), 1.0, 6.0, ((0, 32), (1, 4)))
    buckets_keys = jax.random.split(jax.random.fold_in(splits[1], 1), BATCH * LENGTH // PART)
    buckets_turns = jax.random.permutation(jax.random.fold_in(splits[1], 3), BATCH * LENGTH // PART)
    buckets = jax.vmap(lambda own, number: assign_block(jax.random.fold_in(splits[1], 2), own, number, PART, EXPERTS, 1, SLOT, 1))(buckets_keys, buckets_turns).reshape((BATCH, LENGTH, 1))
    qkv_weight = scatter_about(splits[2], (D, 3 * D), D ** -0.5, 0.21875, ((0, 128),))
    output_weight = scatter_about(splits[3], (D, D), (D // 64) ** -0.5, 1.75, ((0, 128),))
    attend_gain = jnp.clip(1.0 + 0.1 * jax.random.normal(splits[4], (D,), jnp.float32), 0.5, 1.5).astype(jnp.bfloat16)
    attend_bias = scatter_about(splits[5], (D,), 0.2, 1.0, ((0, 128),))
    expert_gain = jnp.clip(1.0 + 0.1 * jax.random.normal(splits[6], (D,), jnp.float32), 0.5, 1.5).astype(jnp.bfloat16)
    expert_bias = scatter_about(splits[7], (D,), 0.2, 1.0, ((0, 128),))
    expert_in = scatter_about(splits[8], (EXPERTS, D, FF), D ** -0.5, 0.21875, ((0, 32), (2, 4)))
    expert_out = scatter_about(splits[9], (EXPERTS, FF, D), (FF // 2) ** -0.5, 0.15625, ((0, 32), (1, 4)))
    cotangent = scatter_about(splits[10], (BATCH, LENGTH, D), 1.0, 6.0, ((0, 32), (1, 4)))
    return dict(tokens=tokens, buckets=buckets, qkv_weight=qkv_weight, output_weight=output_weight, attend_gain=attend_gain, attend_bias=attend_bias, expert_gain=expert_gain, expert_bias=expert_bias, expert_in=expert_in, expert_out=expert_out, cotangent=cotangent)


EPSILON = 1e-05
MASKED = -1e+30

@jax.custom_vjp
def low(v):
    return lax.optimization_barrier(v.astype(jnp.bfloat16)).astype(jnp.float32)

@jax.custom_vjp
def low_back(v):
    return v

def low_keep(v):
    return (low(v), None)

def low_pass(kept, grad):
    return (grad,)

def back_keep(v):
    return (v, None)

def back_low(kept, grad):
    return (low(grad),)
low.defvjp(low_keep, low_pass)
low_back.defvjp(back_keep, back_low)

def rounded_both(values):
    return low(low_back(values))

def normalize(values, gain_vec, bias_vec):
    row_mean = lax.optimization_barrier(jnp.mean(values, -1, keepdims=True))
    centered = values - row_mean
    variance = lax.optimization_barrier(jnp.mean(centered * centered, -1, keepdims=True))
    return centered * lax.rsqrt(variance + EPSILON) * gain_vec + bias_vec

def gelu_value(values):
    return 0.5 * values * (1.0 + lax.erf(values * 0.7071067811865476))

def attend_one(members):
    queries, key_rows, value_rows = members
    raw_scores = jnp.einsum('qhd,khd->hqk', queries, key_rows, precision=lax.Precision.HIGHEST) * HEAD_DIM ** (-0.5)
    raw_scores = low_back(raw_scores)
    places = jnp.arange(LENGTH, dtype=jnp.int32)
    allowed = places[None, :] <= places[:, None]
    masked = jnp.where(allowed[None], raw_scores, MASKED)
    row_top = lax.optimization_barrier(jnp.max(masked, -1, keepdims=True))
    weights = jnp.exp(masked - row_top)
    prob_low = low(weights / lax.optimization_barrier(jnp.sum(weights, -1, keepdims=True)))
    return jnp.einsum('hqk,khd->qhd', prob_low, value_rows, precision=lax.Precision.HIGHEST)

def expert_one(members):
    expert_rows, weight_in, weight_out = members
    pre_act = low_back(jnp.dot(expert_rows, weight_in, precision=lax.Precision.HIGHEST))
    activated = low(gelu_value(pre_act))
    return jnp.dot(activated, weight_out, precision=lax.Precision.HIGHEST)

def slot_index(buckets):
    blocks = buckets.reshape(BATCH * N_SEQ, PART)
    onehot = (blocks[:, :, None] == jnp.arange(EXPERTS, dtype=jnp.int32)[None, None, :]).astype(jnp.int32)
    earlier = jnp.cumsum(onehot, axis=1) - onehot
    rank_ids = lax.optimization_barrier(jnp.sum(earlier * onehot, -1))
    block_ids = jnp.arange(BATCH * N_SEQ, dtype=jnp.int32)[:, None]
    return (blocks * (BATCH * N_SEQ * SLOT) + block_ids * SLOT + rank_ids).reshape(-1).astype(jnp.int32)

def block_forward(tokens, qkv_weight, output_weight, attend_gain, attend_bias, expert_gain, expert_bias, expert_in, expert_out, slot_ids):
    normed = low(normalize(tokens, attend_gain, attend_bias))
    mixed_rows = rounded_both(jnp.einsum('bld,de->ble', normed, qkv_weight, precision=lax.Precision.HIGHEST))
    shaped = mixed_rows.reshape(BATCH, LENGTH, 3, HEADS, HEAD_DIM)
    attended = lax.map(jax.checkpoint(attend_one), (shaped[:, :, 0], shaped[:, :, 1], shaped[:, :, 2]))
    attended = rounded_both(attended.reshape(BATCH, LENGTH, D))
    branch = low_back(jnp.einsum('bld,de->ble', attended, output_weight, precision=lax.Precision.HIGHEST))
    middle = tokens + branch
    second = rounded_both(normalize(middle, expert_gain, expert_bias))
    expert_rows = BATCH * N_SEQ * SLOT
    buffer = jnp.zeros((EXPERTS * expert_rows, D), jnp.float32).at[slot_ids].set(second.reshape(-1, D))
    results = lax.map(jax.checkpoint(expert_one), (buffer.reshape(EXPERTS, expert_rows, D), expert_in, expert_out))
    results = rounded_both(results.reshape(-1, D))
    return middle + results[slot_ids].reshape(BATCH, LENGTH, D)

def reference(tokens, buckets, qkv_weight, output_weight, attend_gain, attend_bias, expert_gain, expert_bias, expert_in, expert_out, cotangent):
    slot_ids = slot_index(buckets)
    floats = [member.astype(jnp.float32) for member in (tokens, qkv_weight, output_weight, attend_gain, attend_bias, expert_gain, expert_bias, expert_in, expert_out)]
    result, pullback = jax.vjp(partial(block_forward, slot_ids=slot_ids), *floats)
    gradients = pullback(cotangent.astype(jnp.float32))
    return (result.astype(jnp.bfloat16), gradients[0].astype(jnp.bfloat16), gradients[1], gradients[2], gradients[3], gradients[4], gradients[5], gradients[6], gradients[7], gradients[8])
```

```python
import jax
import jax.numpy as jnp
from jax import lax
from jax.sharding import Mesh
from jax.sharding import PartitionSpec as P

HEAD_DIM = 64
SLOT = 8
EPSILON = 1e-05
MASKED = -1e30
BF = jnp.bfloat16
F32 = jnp.float32

GROUP = ("core", "y")
CHIPS = ("z", "x", "y")
PLANE = ("z", "x")
EVEN = [(k * 4 + y, (y // 2) * 4 + 2 * k + y % 2) for k in range(2) for y in range(4)]
ODD = [(k * 4 + y, (y // 2) * 4 + 2 * k + 1 - y % 2) for k in range(2) for y in range(4)]
EVEN_BACK = [(b, a) for a, b in EVEN]
ODD_BACK = [(b, a) for a, b in ODD]


def dot(a, b, dims):
    return lax.dot_general(a, b, (dims, ((), ())), preferred_element_type=F32)


def nn(a, b):
    return dot(a, b, ((1,), (0,)))


def nt(a, b):
    return dot(a, b, ((1,), (1,)))


def tn(a, b):
    return dot(a, b, ((0,), (0,)))


def swap(value):
    return lax.ppermute(value, "core", [(0, 1), (1, 0)])


def ordered(first, one, two):
    return jnp.where(first, one, two), jnp.where(first, two, one)


def gather_sequence(blocks, even):
    mine, other = ordered(even, blocks[0], blocks[1])
    mine, other = lax.ppermute(mine, GROUP, EVEN), lax.ppermute(other, GROUP, ODD)
    low, high = ordered(even, mine, other)
    return jnp.concatenate((low, high), 0)


def scatter_sequence(half, even):
    low, high = half[:256], half[256:]
    mine, other = ordered(even, low, high)
    mine, other = lax.ppermute(mine, GROUP, EVEN_BACK), lax.ppermute(other, GROUP, ODD_BACK)
    return jnp.stack(ordered(even, mine, other))


def whole_sequence(half, first):
    low, high = ordered(first, half, swap(half))
    return jnp.concatenate((low, high), 0)


def standardize(values):
    centered = values - jnp.mean(values, -1, keepdims=True)
    inverse = lax.rsqrt(jnp.mean(centered * centered, -1, keepdims=True) + EPSILON)
    return centered * inverse, inverse


def norm_backward(upstream, standard, inverse, gain_vec):
    scaled = upstream * gain_vec
    inner = (
        scaled
        - jnp.mean(scaled, -1, keepdims=True)
        - standard * jnp.mean(scaled * standard, -1, keepdims=True)
    )
    return inner * inverse, jnp.sum(upstream * standard, 0), jnp.sum(upstream, 0)


def heads_of(value):
    return value.reshape(value.shape[0], -1, HEAD_DIM)


def scores_of(queries, keys):
    length = queries.shape[0]
    raw = jnp.einsum("qhd,khd->hqk", heads_of(queries), heads_of(keys), preferred_element_type=F32)
    places = jnp.arange(length, dtype=jnp.int32)
    return jnp.where((places[None, :] <= places[:, None])[None], raw * HEAD_DIM**-0.5, MASKED)


def attend_forward(mixed):
    queries, keys, values = jnp.split(mixed, 3, -1)
    scores = scores_of(queries, keys)
    top = jnp.max(scores, -1, keepdims=True)
    weights = jnp.exp(scores - top)
    totals = jnp.sum(weights, -1, keepdims=True)
    low = (weights / totals).astype(BF)
    result = jnp.einsum("hqk,khd->qhd", low, heads_of(values), preferred_element_type=F32)
    return result.reshape(queries.shape).astype(BF), top + jnp.log(totals)


def attend_backward(mixed, logs, upstream):
    queries, keys, values = jnp.split(mixed, 3, -1)
    probs = jnp.exp(scores_of(queries, keys) - logs)
    up = heads_of(upstream)
    prob_grad = jnp.einsum("qhd,khd->hqk", up, heads_of(values), preferred_element_type=F32)
    value_grad = jnp.einsum("hqk,qhd->khd", probs.astype(BF), up, preferred_element_type=F32)
    row_dot = jnp.sum(prob_grad * probs, -1, keepdims=True)
    score_grad = (probs * (prob_grad - row_dot)).astype(BF)
    scale = HEAD_DIM**-0.5
    query_grad = scale * jnp.einsum("hqk,khd->qhd", score_grad, heads_of(keys), preferred_element_type=F32)
    key_grad = scale * jnp.einsum("hqk,qhd->khd", score_grad, heads_of(queries), preferred_element_type=F32)
    parts = (query_grad, key_grad, value_grad)
    return jnp.concatenate([part.reshape(queries.shape) for part in parts], -1).astype(BF)


def gelu_parts(values):
    cumulative = 0.5 * (1.0 + lax.erf(values * 0.7071067811865476))
    slope = cumulative + values * jnp.exp(-0.5 * values * values) * 0.3989422804014327
    return values * cumulative, slope


def slot_matrix(ids):
    blocks = ids.reshape(2, 256)
    same = blocks[:, :, None] == blocks[:, None, :]
    places = jnp.arange(256, dtype=jnp.int32)
    rank = jnp.sum((same & (places[None, :] < places[:, None])).astype(jnp.int32), -1)
    slots = blocks * (2 * SLOT) + jnp.arange(2, dtype=jnp.int32)[:, None] * SLOT + rank
    return (jnp.arange(1024, dtype=jnp.int32)[:, None] == slots.reshape(1, 512)).astype(BF)


def to_experts(rows, slots):
    return lax.all_to_all(nn(slots, rows).astype(BF).reshape(64, 16, -1), CHIPS, 0, 0, tiled=True).reshape(1024, -1)


def from_experts(rows, slots):
    back = lax.all_to_all(rows.reshape(64, 16, -1), CHIPS, 0, 0, tiled=True).reshape(1024, -1)
    return tn(slots, back)


def gather_projections(qkv, out, vectors, first):
    columns = jnp.stack(vectors, -1)
    columns = jnp.pad(columns, ((0, 0), (0, 128 - len(vectors))))
    qkv, out = qkv.reshape(6, 3, 2, 384), out.reshape(6, 2, 384)
    halves = jnp.stack(
        [jnp.concatenate((qkv[:, :, k].reshape(6, 1152), out[:, k], columns), -1) for k in range(2)]
    )
    sent = jnp.broadcast_to(halves[:, None], (2, 4, 6, 1664)).reshape(8, 6, 1664)
    rows = lax.all_to_all(sent, GROUP, 0, 0, tiled=True).reshape(1, 48, 1664)
    sent = jnp.broadcast_to(rows, (16, 48, 1664))
    return lax.all_to_all(sent, PLANE, 0, 0, tiled=True).reshape(768, 1664)


def reduce_projections(grads):
    got = lax.all_to_all(grads.reshape(16, 48, 1664), PLANE, 0, 0, tiled=True)
    rows = jnp.sum(got.astype(F32), 0).reshape(8, 6, 1664)
    got = lax.all_to_all(rows, GROUP, 0, 0, tiled=True).reshape(2, 4, 6, 1664)
    rows = jnp.sum(got, 1)
    qkv = rows[:, :, :1152].reshape(2, 6, 3, 384).transpose(1, 2, 0, 3).reshape(6, 2304)
    out = rows[:, :, 1152:1536].transpose(1, 0, 2).reshape(6, 768)
    vectors = jnp.sum(rows[:, :, 1536:1540], 0)
    return qkv, out, vectors


def local(
    tokens,
    buckets,
    qkv_weight,
    output_weight,
    attend_gain,
    attend_bias,
    expert_gain,
    expert_bias,
    expert_in,
    expert_out,
    cotangent,
):
    even = lax.axis_index("y") % 2 == 0
    first = lax.axis_index("core") == 0
    projections = gather_projections(
        qkv_weight, output_weight, (attend_gain, attend_bias, expert_gain, expert_bias), first
    )
    inputs = gather_sequence(tokens, even).astype(F32)
    upstream_low = gather_sequence(cotangent, even)
    slots = slot_matrix(gather_sequence(buckets, even).reshape(512))

    experts = jnp.stack((expert_in, expert_out), 1)
    mine, other = ordered(even, experts[0], experts[1])
    block_a, block_b = lax.ppermute(mine, GROUP, EVEN), lax.ppermute(other, GROUP, ODD)
    block_c, block_d = swap(block_a), swap(block_b)
    blocks = (block_a, block_b, block_c, block_d)
    weight_in = jnp.concatenate([block[0] for block in blocks], 1)
    weight_out = jnp.concatenate([block[1] for block in blocks], 0)
    grad_rows = to_experts(upstream_low, slots)

    qkv_half = projections[:, :1152]
    out_half = projections[:, 1152:1536]
    vectors = projections[:, 1536:1540].astype(F32).T
    gain_one, bias_one, gain_two, bias_two = (vectors[i : i + 1] for i in range(4))
    out_full = jnp.concatenate(ordered(first, out_half, swap(out_half)), 1)

    standard_one, inverse_one = standardize(inputs)
    normed = (standard_one * gain_one + bias_one).astype(BF)
    normed = whole_sequence(normed, first)
    mixed = nn(normed, qkv_half).astype(BF)
    heads, logs = attend_forward(mixed)
    own, other = ordered(first, heads[:512], heads[512:])
    attended = jnp.concatenate(ordered(first, own, swap(other)), 1)
    middle = inputs + nn(attended, out_full)
    standard_two, inverse_two = standardize(middle)
    second = (standard_two * gain_two + bias_two).astype(BF)

    rows = to_experts(second, slots)
    activated, slope = gelu_parts(nn(rows, weight_in))
    activated = activated.astype(BF)
    pre_grad = (nt(grad_rows, weight_out) * slope).astype(BF)
    row_grad = nt(pre_grad, weight_in).astype(BF)
    second_grad = from_experts(row_grad, slots)
    result = nn(activated, weight_out).astype(BF)
    block_out = (middle + from_experts(result, slots)).astype(BF)
    block_out = scatter_sequence(block_out, even)

    in_grad = tn(rows, pre_grad)
    out_grad = tn(activated, grad_rows)
    parts = [
        jnp.stack((in_grad[:, 768 * i : 768 * i + 768], out_grad[768 * i : 768 * i + 768])) for i in range(4)
    ]
    grad_a = (parts[0] + swap(parts[2].astype(BF)).astype(F32)).astype(BF)
    grad_b = (parts[1] + swap(parts[3].astype(BF)).astype(F32)).astype(BF)
    grad_a, grad_b = lax.ppermute(grad_a, GROUP, EVEN_BACK), lax.ppermute(grad_b, GROUP, ODD_BACK)
    expert_grads = jnp.stack(ordered(even, grad_a, grad_b)).astype(F32)

    upstream = upstream_low.astype(F32)
    norm_grad, gain_two_grad, bias_two_grad = norm_backward(second_grad, standard_two, inverse_two, gain_two)
    middle_grad = upstream + norm_grad
    branch_grad = middle_grad.astype(BF)
    out_partial = tn(attended, branch_grad)
    keep, give = ordered(first, out_partial[:, :384], out_partial[:, 384:])
    out_total = (keep + swap(give.astype(BF)).astype(F32)).astype(BF)
    attended_grad = nt(branch_grad, out_full).astype(BF)
    keep, give = ordered(first, attended_grad[:, :384], attended_grad[:, 384:])
    heads_grad = jnp.concatenate(ordered(first, keep, swap(give)), 0)
    mixed_grad = attend_backward(mixed, logs, heads_grad)
    qkv_total = tn(normed, mixed_grad).astype(BF)
    normed_partial = nt(mixed_grad, qkv_half)
    keep, give = ordered(first, normed_partial[:512], normed_partial[512:])
    normed_grad = keep + swap(give.astype(BF)).astype(F32)
    first_grad, gain_one_grad, bias_one_grad = norm_backward(normed_grad, standard_one, inverse_one, gain_one)
    token_grad = scatter_sequence((middle_grad + first_grad).astype(BF), even)

    columns = jnp.stack((gain_one_grad, bias_one_grad, gain_two_grad, bias_two_grad), -1).astype(BF)
    columns = jnp.pad(columns, ((0, 0), (0, 124)))
    qkv_grad, outproj_grad, shares = reduce_projections(
        jnp.concatenate((qkv_total, out_total, columns), -1)
    )
    return (
        block_out,
        token_grad,
        qkv_grad,
        outproj_grad,
        shares[:, 0],
        shares[:, 1],
        shares[:, 2],
        shares[:, 3],
        expert_grads[:, 0],
        expert_grads[:, 1],
    )


def solution(mesh):
    fine = Mesh(mesh.devices.reshape(4, 4, 2, 4), ("z", "x", "core", "y"))
    dp, every = ("z", "x", "core"), ("z", "x", "core", "y")
    rows = P(dp, "y", None)
    in_specs = (
        rows,
        rows,
        P(every, None),
        P(every, None),
        P(every),
        P(every),
        P(every),
        P(every),
        P(dp, None, "y"),
        P(dp, "y", None),
        rows,
    )
    out_specs = (
        rows,
        rows,
        P(every, None),
        P(every, None),
        P(every),
        P(every),
        P(every),
        P(every),
        P(dp, None, "y"),
        P(dp, "y", None),
    )
    return jax.shard_map(local, mesh=fine, in_specs=in_specs, out_specs=out_specs, check_vma=False)
```

```python
import functools

import jax
import jax.numpy as jnp
from jax import lax
from jax.experimental import pallas as pl
from jax.experimental.pallas import tpu as pltpu
from jax.sharding import Mesh
from jax.sharding import PartitionSpec as P

HEAD_DIM = 64
SLOT = 8
TILE = 256
EPSILON = 1e-05
MASKED = -1e30
BF = jnp.bfloat16
F32 = jnp.float32

GROUP = ("core", "y")
CHIPS = ("z", "x", "y")
PLANE = ("z", "x")
EVEN = [(k * 4 + y, (1 - y // 2) * 4 + 2 * k + y % 2) for k in range(2) for y in range(4)]
ODD = [(k * 4 + y, (1 - y // 2) * 4 + 2 * k + 1 - y % 2) for k in range(2) for y in range(4)]
EVEN_BACK = [(b, a) for a, b in EVEN]
ODD_BACK = [(b, a) for a, b in ODD]


def dot(a, b, dims):
    return lax.dot_general(a, b, (dims, ((), ())), preferred_element_type=F32)


def nn(a, b):
    return dot(a, b, ((1,), (0,)))


def nt(a, b):
    return dot(a, b, ((1,), (1,)))


def tn(a, b):
    return dot(a, b, ((0,), (0,)))


def swap(value):
    return lax.ppermute(value, "core", [(0, 1), (1, 0)])


def ordered(first, one, two):
    return jnp.where(first, one, two), jnp.where(first, two, one)


def gather_sequence(blocks, even):
    return gather_ordered(*ordered(even, blocks[0], blocks[1]), even)


def gather_ordered(mine, other, even):
    mine, other = lax.ppermute(mine, GROUP, EVEN), lax.ppermute(other, GROUP, ODD)
    low, high = ordered(even, mine, other)
    return jnp.concatenate((low, high), 0)


def scatter_sequence(half, even):
    low, high = half[:256], half[256:]
    mine, other = ordered(even, low, high)
    mine, other = lax.ppermute(mine, GROUP, EVEN_BACK), lax.ppermute(other, GROUP, ODD_BACK)
    return jnp.stack(ordered(even, mine, other))


def together(*values):
    return lax.optimization_barrier(values)


def standardize(values):
    centered = values - jnp.mean(values, -1, keepdims=True)
    inverse = lax.rsqrt(jnp.mean(centered * centered, -1, keepdims=True) + EPSILON)
    return centered * inverse, inverse


def norm_backward(upstream, standard, inverse, gain_vec):
    scaled = upstream * gain_vec
    return inverse * (
        scaled
        - jnp.mean(scaled, -1, keepdims=True)
        - standard * jnp.mean(scaled * standard, -1, keepdims=True)
    )


def sum_rows(values):
    return jnp.sum(values, 0, keepdims=True)


def call(kernel, grid, in_specs, out_specs, out_shape, scratch=(), vmem=28):
    return pl.pallas_call(
        kernel,
        grid=grid,
        in_specs=in_specs,
        out_specs=out_specs,
        out_shape=out_shape,
        scratch_shapes=scratch,
        compiler_params=pltpu.CompilerParams(vmem_limit_bytes=vmem * 2**20),
        cost_estimate=pl.CostEstimate(flops=100_000_000, bytes_accessed=2**16, transcendentals=0),
    )


WHOLE = pl.BlockSpec(memory_space=pltpu.VMEM)
SCALAR = pl.BlockSpec(memory_space=pltpu.SMEM)


def shape(dtype, *sizes):
    return jax.ShapeDtypeStruct(sizes, dtype)


def at_core(core, extent):
    return pl.ds(pl.multiple_of(core * extent, 128), extent)


def project_kernel(core_ref, own_ref, other_ref, weight_ref, normed_ref, mixed_ref, vector_ref, out_ref):
    core = core_ref[0]
    row = lax.broadcasted_iota(jnp.int32, (8, 128), 0)
    col = lax.broadcasted_iota(jnp.int32, (8, 128), 1)
    vectors = nt((row == col).astype(BF), weight_ref[:, 1536:])
    vector_ref[...] = vectors
    out_ref[...] = weight_ref[:, 1152:1536]
    for half, ref in ((1 - core, own_ref), (core, other_ref)):
        for i in range(2):
            standard, _ = standardize(ref[TILE * i : TILE * i + TILE, :768].astype(F32))
            normed = (standard * vectors[0:1] + vectors[1:2]).astype(BF)
            normed_ref[pl.ds(pl.multiple_of(half * 512 + TILE * i, TILE), TILE), :] = normed
    mixed_ref[...] = nn(normed_ref[...], weight_ref[:, :1152]).astype(BF)


def project(core, own, other, projections):
    return call(
        project_kernel,
        (),
        [SCALAR, WHOLE, WHOLE, WHOLE],
        [WHOLE] * 4,
        [shape(BF, 1024, 768), shape(BF, 1024, 1152), shape(F32, 8, 768), shape(BF, 768, 384)],
    )(core, own, other, projections)


def leave_kernel(
    core_ref, own_ref, other_ref, mine_ref, theirs_ref, token_ref, vector_ref, slot_ref,
    middle_ref, attended_ref, sent_ref,
):
    core = core_ref[0]
    here, there = at_core(core, 384), at_core(1 - core, 384)
    attended_ref[:, here] = own_ref[...]
    attended_ref[:, there] = other_ref[...]
    middle_ref[:, here] = nn(attended_ref[...], mine_ref[...])
    middle_ref[:, there] = nn(attended_ref[...], theirs_ref[...])
    middle = token_ref[:, :768].astype(F32) + middle_ref[...]
    middle_ref[...] = middle
    second = (standardize(middle)[0] * vector_ref[2:3, :] + vector_ref[3:4, :]).astype(BF)
    slots = lax.broadcasted_iota(jnp.int32, (1024, 512), 0) == slot_ref[...]
    sent_ref[...] = nn(slots.astype(BF), second).astype(BF)


def leave(core, own, other, mine, theirs, tokens, vectors, slots):
    return call(
        leave_kernel,
        (),
        [SCALAR] + [WHOLE] * 7,
        [WHOLE] * 3,
        [shape(F32, 512, 768), shape(BF, 512, 768), shape(BF, 1024, 768)],
    )(core, own, other, mine, theirs, tokens, vectors, slots.reshape(1, 512))


def enter_kernel(
    core_ref, back_ref, middle_ref, up_ref, mine_ref, theirs_ref, vector_ref, slot_ref,
    grad_ref, low_ref, keep_ref, give_ref, sums_ref,
):
    core = core_ref[0]
    here, there = at_core(core, 384), at_core(1 - core, 384)
    slots = lax.broadcasted_iota(jnp.int32, (512, 1024), 1) == slot_ref[...]
    second_grad = nn(slots.astype(BF), back_ref[...])
    standard, inverse = standardize(middle_ref[...])
    sums_ref[...] = jnp.zeros_like(sums_ref)
    sums_ref[2:3, :] = sum_rows(second_grad * standard)
    sums_ref[3:4, :] = sum_rows(second_grad)
    grad = up_ref[...].astype(F32) + norm_backward(second_grad, standard, inverse, vector_ref[2:3, :])
    grad_ref[...] = grad
    low_ref[...] = grad.astype(BF)
    for ref, rows in ((keep_ref, here), (give_ref, there)):
        total = nt(low_ref[:, here], mine_ref[rows, :]) + nt(low_ref[:, there], theirs_ref[rows, :])
        ref[...] = total.astype(BF)


def enter(core, back_rows, middle, upstream, mine, theirs, vectors, slots):
    return call(
        enter_kernel,
        (),
        [SCALAR] + [WHOLE] * 7,
        [WHOLE] * 5,
        [
            shape(F32, 512, 768),
            shape(BF, 512, 768),
            shape(BF, 512, 384),
            shape(BF, 512, 384),
            shape(F32, 8, 768),
        ],
    )(core, back_rows, middle, upstream, mine, theirs, vectors, slots.reshape(512, 1))


def finish_kernel(
    keep_ref, got_ref, token_ref, grad_ref, vector_ref, sums_ref, normed_ref, mixed_ref, kept_ref, given_ref,
    out_ref, share_ref,
):
    normed_grad = keep_ref[...] + got_ref[...].astype(F32)
    standard, inverse = standardize(token_ref[:, :768].astype(F32))
    grad = grad_ref[...] + norm_backward(normed_grad, standard, inverse, vector_ref[0:1, :])
    out_ref[...] = grad.astype(BF)
    place = lax.broadcasted_iota(jnp.int32, (8, 768), 0)
    sums = jnp.where(place == 0, sum_rows(normed_grad * standard), sums_ref[...])
    sums = jnp.where(place == 1, sum_rows(normed_grad), sums)
    row = lax.broadcasted_iota(jnp.int32, (8, 128), 0)
    col = lax.broadcasted_iota(jnp.int32, (8, 128), 1)
    share_ref[:, 1536:] = tn(sums.astype(BF), (row == col).astype(BF)).astype(BF)
    share_ref[:, 1152:1536] = (kept_ref[...] + given_ref[...].astype(F32)).astype(BF)
    share_ref[:, :1152] = tn(normed_ref[...], mixed_ref[...]).astype(BF)


def finish(*values):
    return call(
        finish_kernel,
        (),
        [WHOLE] * 10,
        [WHOLE] * 2,
        [shape(BF, 512, 768), shape(BF, 768, 1664)],
    )(*values)


def head_lanes(head):
    lane = lax.broadcasted_iota(jnp.int32, (TILE, 128), 1)
    return lane < HEAD_DIM if head == 0 else lane >= HEAD_DIM


def one_head(value, head):
    return jnp.where(head_lanes(head), value, jnp.zeros_like(value))


def attend_forward_kernel(q_ref, k_ref, v_ref, out_ref, log_ref):
    row = lax.broadcasted_iota(jnp.int32, (TILE, TILE), 0)
    col = lax.broadcasted_iota(jnp.int32, (TILE, TILE), 1)
    for i in range(q_ref.shape[0] // TILE):
        rows = pl.ds(i * TILE, TILE)
        queries = q_ref[rows, :] * jnp.asarray(HEAD_DIM**-0.5, BF)
        outs, logs = [], []
        for head in range(2):
            part = one_head(queries, head)
            scores = [nt(part, k_ref[pl.ds(j * TILE, TILE), :]) for j in range(i + 1)]
            scores[i] = jnp.where(col <= row, scores[i], MASKED)
            top = functools.reduce(jnp.maximum, [jnp.max(s, axis=1, keepdims=True) for s in scores])
            weights = [jnp.exp(s - top) for s in scores]
            total = functools.reduce(jnp.add, [jnp.sum(w, axis=1, keepdims=True) for w in weights])
            out = functools.reduce(
                jnp.add, [nn(weights[j].astype(BF), v_ref[pl.ds(j * TILE, TILE), :]) for j in range(i + 1)]
            )
            outs.append(out * (1.0 / total))
            logs.append(jnp.broadcast_to(top + jnp.log(total), (TILE, 128)))
        out_ref[rows, :] = jnp.where(head_lanes(0), outs[0], outs[1]).astype(BF)
        log_ref[rows, :] = jnp.where(head_lanes(0), logs[0], logs[1])


def attend_forward(mixed):
    length, width = mixed.shape
    pairs = width // 384

    def at(shift):
        return pl.BlockSpec((length, 128), lambda p: (0, p + shift))

    return call(
        attend_forward_kernel,
        (pairs,),
        [at(0), at(pairs), at(2 * pairs)],
        [at(0), at(0)],
        [
            jax.ShapeDtypeStruct((length, 128 * pairs), BF),
            jax.ShapeDtypeStruct((length, 128 * pairs), F32),
        ],
    )(mixed, mixed, mixed)


def attend_backward_kernel(
    core_ref, q_ref, k_ref, v_ref, o_ref, log_ref, g_ref, weight_ref, out_ref, keep_ref, give_ref, k_sum, v_sum
):
    def columns(part):
        start = part * (out_ref.shape[1] // 3) + pl.program_id(0) * 128
        return pl.ds(pl.multiple_of(start, 128), 128)

    key = lax.broadcasted_iota(jnp.int32, (TILE, TILE), 0)
    query = lax.broadcasted_iota(jnp.int32, (TILE, TILE), 1)
    k_sum[...] = jnp.zeros_like(k_sum)
    v_sum[...] = jnp.zeros_like(v_sum)
    for i in range(q_ref.shape[0] // TILE):
        rows = pl.ds(i * TILE, TILE)
        queries = q_ref[rows, :] * jnp.asarray(HEAD_DIM**-0.5, BF)
        up = g_ref[rows, :]
        product = (up.astype(F32) * o_ref[rows, :].astype(F32)).T
        logs = log_ref[rows, :].T
        sums = []
        for head in range(2):
            q_part, g_part = one_head(queries, head), one_head(up, head)
            row_dot = jnp.sum(product[64 * head : 64 * head + 64], axis=0, keepdims=True)
            log_row = logs[64 * head : 64 * head + 1]
            total = None
            for j in range(i + 1):
                cols = pl.ds(j * TILE, TILE)
                scores = nt(k_ref[cols, :], q_part)
                if j == i:
                    scores = jnp.where(key <= query, scores, MASKED)
                probs = jnp.exp(scores - log_row)
                prob_grad = nt(v_ref[cols, :], g_part)
                score_grad = (probs * (prob_grad - row_dot)).astype(BF)
                v_sum[cols, :] += nn(probs.astype(BF), g_part)
                k_sum[cols, :] += nn(score_grad, q_part)
                term = tn(score_grad, k_ref[cols, :])
                total = term if total is None else total + term
            sums.append(total)
        grad = jnp.where(head_lanes(0), sums[0], sums[1]) * HEAD_DIM**-0.5
        out_ref[rows, columns(0)] = grad.astype(BF)
    out_ref[:, columns(1)] = k_sum[...].astype(BF)
    out_ref[:, columns(2)] = v_sum[...].astype(BF)

    @pl.when(pl.program_id(0) == pl.num_programs(0) - 1)
    def _():
        weight, core = weight_ref[:, : out_ref.shape[1]], core_ref[0]
        give_ref[...] = nt(out_ref[at_core(core, 512), :], weight).astype(BF)
        keep_ref[...] = nt(out_ref[at_core(1 - core, 512), :], weight)


def attend_backward(core, mixed, attended, logs, upstream, projections):
    length, width = mixed.shape
    pairs = width // 384

    def at(shift):
        return pl.BlockSpec((length, 128), lambda p: (0, p + shift))

    def whole(*sizes):
        return pl.BlockSpec(sizes, lambda p: (0, 0))

    return call(
        attend_backward_kernel,
        (pairs,),
        [SCALAR, at(0), at(pairs), at(2 * pairs), at(0), at(0), at(0), whole(768, 1664)],
        [whole(length, width), whole(512, 768), whole(512, 768)],
        [shape(BF, length, width), shape(F32, 512, 768), shape(BF, 512, 768)],
        [pltpu.VMEM((length, 128), F32)] * 2,
    )(core, mixed, mixed, mixed, attended, logs, upstream, projections)


def of_block(which):
    return pl.BlockSpec((1, 768, 768), lambda i: (which, 0, 0))


def rows_of(count, width):
    return pl.BlockSpec((count, width), lambda i: (i, 0))


def act_grad_kernel(grad_ref, *refs):
    for i, block in enumerate(refs[:4]):
        refs[4][:, 768 * i : 768 * i + 768] = nt(grad_ref[...], block[0]).astype(BF)


def act_grads(grads, blocks):
    count = grads.shape[0]
    return call(
        act_grad_kernel,
        (4,),
        [rows_of(count // 4, 768)] + [of_block(1)] * 4,
        rows_of(count // 4, 3072),
        jax.ShapeDtypeStruct((count, 3072), BF),
        vmem=56,
    )(grads, *blocks)


def expert_kernel(row_ref, grad_ref, *refs):
    act_ref, pre_ref, out_ref = refs[4:]
    rows = row_ref[...]
    total = None
    for i, block in enumerate(refs[:4]):
        cols = slice(768 * i, 768 * i + 768)
        weight = block[0]
        pre = nn(rows, weight)
        cumulative = 0.5 * (1.0 + lax.erf(pre * 0.7071067811865476))
        act_ref[:, cols] = (pre * cumulative).astype(BF)
        slope = cumulative + pre * jnp.exp(-0.5 * pre * pre) * 0.3989422804014327
        grad = (grad_ref[:, cols].astype(F32) * slope).astype(BF)
        pre_ref[:, cols] = grad
        term = nt(grad, weight)
        total = term if total is None else total + term
    out_ref[...] = total.astype(BF)


def expert(rows, act_grad, blocks):
    count = rows.shape[0]
    wide = jax.ShapeDtypeStruct((count, 3072), BF)
    return call(
        expert_kernel,
        (4,),
        [rows_of(count // 4, 768), rows_of(count // 4, 3072)] + [of_block(0)] * 4,
        [rows_of(count // 4, 3072), rows_of(count // 4, 3072), rows_of(count // 4, 768)],
        [wide, wide, jax.ShapeDtypeStruct((count, 768), BF)],
        vmem=56,
    )(rows, act_grad, *blocks)


def result_kernel(act_ref, *refs):
    terms = [nn(act_ref[:, 768 * i : 768 * i + 768], refs[i][0]) for i in range(4)]
    refs[4][...] = functools.reduce(jnp.add, terms).astype(BF)


def expert_results(activated, blocks):
    count = activated.shape[0]
    return call(
        result_kernel,
        (4,),
        [rows_of(count // 4, 3072)] + [of_block(1)] * 4,
        rows_of(count // 4, 768),
        jax.ShapeDtypeStruct((count, 768), BF),
        vmem=56,
    )(activated, *blocks)


def weight_grad_kernel(row_ref, grad_ref, act_ref, pre_ref, *refs):
    one, two = tn(row_ref[...], pre_ref[...]), tn(act_ref[...], grad_ref[...])
    if len(refs) == 1:
        refs[0][0, 0] = one.astype(BF)
        refs[0][0, 1] = two.astype(BF)
        return
    one, two = one + refs[0][0, 0].astype(F32), two + refs[0][0, 1].astype(F32)
    for step, ref in enumerate(refs[1:]):

        @pl.when(pl.program_id(0) == step)
        def _():
            ref[0] = one.astype(BF)
            ref[1] = two.astype(BF)


def weight_grads(rows, grads, activated, pre_grad, start, *others):
    count = rows.shape[0]
    whole = pl.BlockSpec((count, 768), lambda i: (0, 0))
    block = pl.BlockSpec((count, 768), lambda i: (0, i + start))
    both = pl.BlockSpec((1, 2, 768, 768), lambda i: (i, 0, 0, 0))
    single = pl.BlockSpec((2, 768, 768), lambda i: (0, 0, 0))
    return call(
        weight_grad_kernel,
        (2,),
        [whole, whole, block, block] + [both] * len(others),
        [single, single] if others else both,
        [shape(BF, 2, 768, 768)] * 2 if others else shape(BF, 2, 2, 768, 768),
        vmem=56,
    )(rows, grads, activated, pre_grad, *others)


def place_kernel(even_ref, a_ref, b_ref, in_ref, out_ref):
    from_a = (pl.program_id(1) == 0) == (even_ref[0] == 1)

    @pl.when(from_a)
    def _():
        in_ref[0] = a_ref[0].astype(F32)
        out_ref[0] = a_ref[1].astype(F32)

    @pl.when(jnp.logical_not(from_a))
    def _():
        in_ref[0] = b_ref[0].astype(F32)
        out_ref[0] = b_ref[1].astype(F32)


def place_expert_grads(even, grad_a, grad_b):
    taken = pl.BlockSpec((2, 256, 768), lambda i, e: (0, i, 0))
    given = pl.BlockSpec((1, 256, 768), lambda i, e: (e, i, 0))
    return call(
        place_kernel,
        (3, 2),
        [pl.BlockSpec(memory_space=pltpu.SMEM), taken, taken],
        [given, given],
        [jax.ShapeDtypeStruct((2, 768, 768), F32)] * 2,
    )(even.astype(jnp.int32).reshape(1), grad_a, grad_b)


def slots_of(ids):
    blocks = ids.reshape(2, 256)
    same = blocks[:, :, None] == blocks[:, None, :]
    places = jnp.arange(256, dtype=jnp.int32)
    rank = jnp.sum((same & (places[None, :] < places[:, None])).astype(jnp.int32), -1)
    slots = blocks * (2 * SLOT) + jnp.arange(2, dtype=jnp.int32)[:, None] * SLOT + rank
    return slots.reshape(512)


def slot_rows(rows, slots):
    matrix = jnp.arange(1024, dtype=jnp.int32)[:, None] == slots[None, :]
    return nn(matrix.astype(BF), rows).astype(BF)


def align_rows(rows, first):
    rows = rows.reshape(16, 2, 2, 2, 8, 768)
    keep, give = ordered(first, rows[:, 1], rows[:, 0])
    low, high = ordered(first, keep, swap(give))
    return jnp.stack((low, high), 1).transpose(0, 1, 3, 2, 4, 5).reshape(1024, 768)


def token_rows(rows, slots):
    matrix = slots[:, None] == jnp.arange(1024, dtype=jnp.int32)[None, :]
    return nn(matrix.astype(BF), rows)


def exchange(rows):
    return lax.all_to_all(rows.reshape(64, 16, -1), CHIPS, 0, 0, tiled=True).reshape(1024, -1)


def gather_group(qkv, out, vectors):
    columns = tn(jnp.stack(vectors), jnp.eye(4, 128, dtype=BF)).astype(BF)
    qkv, out = qkv.reshape(6, 3, 2, 384), out.reshape(6, 2, 384)
    halves = jnp.stack(
        [jnp.concatenate((qkv[:, :, k].reshape(6, 1152), out[:, k], columns), -1) for k in range(2)]
    )
    sent = jnp.broadcast_to(halves[:, None], (2, 4, 6, 1664)).reshape(8, 6, 1664)
    return lax.all_to_all(sent, GROUP, 0, 0, tiled=True).reshape(48, 1664)


def reduce_plane(grads):
    got = lax.all_to_all(grads.reshape(16, 48, 1664), PLANE, 0, 0, tiled=True)
    return jnp.sum(got.astype(F32), 0)


def reduce_projections(rows, first):
    rows = rows.reshape(2, 4, 6, 1664)
    place = lax.axis_index("y")

    def part(of):
        return lax.dynamic_slice_in_dim(rows, of % 4, 1, 1).reshape(2, 6, 1664)

    total = part(place)
    for shift in (2, 1, 3):
        total = total + lax.ppermute(part(place + shift), "y", [(i, (i + shift) % 4) for i in range(4)])
    keep, give = ordered(first, total[0], total[1])
    both = ordered(first, keep, swap(give))
    qkv = jnp.stack([half[:, :1152].reshape(6, 3, 384) for half in both], 2).reshape(6, 2304)
    out = jnp.concatenate([half[:, 1152:1536] for half in both], 1)
    return qkv, out, both[0][:, 1536:1540] + both[1][:, 1536:1540]


def local(
    tokens,
    buckets,
    qkv_weight,
    output_weight,
    attend_gain,
    attend_bias,
    expert_gain,
    expert_bias,
    expert_in,
    expert_out,
    cotangent,
):
    even = lax.axis_index("y") % 2 == 0
    first = lax.axis_index("core") == 0
    core = lax.axis_index("core").astype(jnp.int32).reshape(1)

    def halves(value, extent, axis=0):
        return ordered(
            first,
            lax.slice_in_dim(value, 0, extent, axis=axis),
            lax.slice_in_dim(value, extent, 2 * extent, axis=axis),
        )

    rows = gather_group(qkv_weight, output_weight, (attend_gain, attend_bias, expert_gain, expert_bias))
    sent = jnp.broadcast_to(rows, (16, 48, 1664))
    projections = lax.all_to_all(sent, PLANE, 0, 0, tiled=True).reshape(768, 1664)
    packed = jnp.pad(buckets.astype(BF), ((0, 0), (0, 0), (0, 127)))
    packed = jnp.concatenate((tokens, packed), -1)
    grad_slots = slot_rows(cotangent.reshape(512, 768), slots_of(buckets.reshape(512)))
    packed, grad_slots = together(packed, grad_slots)
    packed, expert_in, expert_out = together(packed, expert_in, expert_out)
    packed = gather_sequence(packed, even)
    slots = slots_of(packed[:, 768].astype(jnp.int32))
    grad_rows = exchange(grad_slots)

    experts = jnp.stack((expert_in, expert_out), 1)
    mine, other = ordered(even, experts[0], experts[1])
    block_a, block_b = lax.ppermute(mine, GROUP, EVEN), lax.ppermute(other, GROUP, ODD)

    normed, mixed, vectors, out_mine = project(core, packed, swap(packed[:, :768]), projections)
    out_theirs = swap(out_mine)
    heads, logs = attend_forward(mixed)
    give, keep = halves(heads, 512)
    middle, attended, sent = leave(core, keep, swap(give), out_mine, out_theirs, packed, vectors, slots)

    sent, block_a, block_b, grad_rows = together(sent, block_a, block_b, grad_rows)
    grad_rows = align_rows(grad_rows, first)
    blocks = (block_a, block_b, swap(block_a), swap(block_b))
    rows = exchange(sent)
    act_grad, *upstream = together(act_grads(grad_rows, blocks), *ordered(even, cotangent[0], cotangent[1]))
    upstream = gather_ordered(*upstream, even)
    activated, pre_grad, row_grad = expert(rows, act_grad, blocks)
    row_grad, upstream = together(row_grad, upstream)
    back_rows = exchange(row_grad)
    result = expert_results(activated, blocks)
    result, pre_grad = together(result, pre_grad)
    made = (rows, grad_rows, activated, pre_grad)
    theirs = weight_grads(*made, 2)
    back_rows, theirs, result = together(back_rows, theirs, result)
    result_rows = exchange(result)
    grad_a, grad_b = weight_grads(*made, 0, swap(theirs))
    back_rows, grad_a, grad_b = together(back_rows, grad_a, grad_b)
    grad_a, grad_b = lax.ppermute(grad_a, GROUP, EVEN_BACK), lax.ppermute(grad_b, GROUP, ODD_BACK)

    middle_grad, branch_grad, keep, give, sums = enter(
        core, back_rows, middle, upstream, out_mine, out_theirs, vectors, slots
    )
    got = swap(give)
    heads_grad = jnp.concatenate(ordered(first, got, keep), 0)
    heads_grad, result_rows = together(heads_grad, result_rows)
    mixed_grad, keep, give = attend_backward(core, mixed, heads, logs, heads_grad, projections)

    out_keep, out_give = halves(tn(attended, branch_grad), 384, 1)
    out_got = swap(out_give.astype(BF))
    token_grad, shares = finish(
        keep, swap(give), packed, middle_grad, vectors, sums, normed, mixed_grad, out_keep, out_got
    )
    shares, grad_a, grad_b = together(shares, grad_a, grad_b)
    token_grad = scatter_sequence(token_grad, even)
    block_out = scatter_sequence((middle + token_rows(result_rows, slots)).astype(BF), even)
    expert_in_grad, expert_out_grad = place_expert_grads(even, grad_a, grad_b)
    summed = reduce_plane(shares)
    summed, expert_in_grad, expert_out_grad = together(summed, expert_in_grad, expert_out_grad)
    qkv_grad, outproj_grad, shares = reduce_projections(summed, first)
    return (
        block_out,
        token_grad,
        qkv_grad,
        outproj_grad,
        shares[:, 0],
        shares[:, 1],
        shares[:, 2],
        shares[:, 3],
        expert_in_grad,
        expert_out_grad,
    )


def solution(mesh):
    fine = Mesh(mesh.devices.reshape(4, 4, 2, 4), ("z", "x", "core", "y"))
    dp, every = ("z", "x", "core"), ("z", "x", "core", "y")
    rows = P(dp, "y", None)
    in_specs = (
        rows,
        rows,
        P(every, None),
        P(every, None),
        P(every),
        P(every),
        P(every),
        P(every),
        P(dp, None, "y"),
        P(dp, "y", None),
        rows,
    )
    out_specs = (
        rows,
        rows,
        P(every, None),
        P(every, None),
        P(every),
        P(every),
        P(every),
        P(every),
        P(dp, None, "y"),
        P(dp, "y", None),
    )
    return jax.shard_map(local, mesh=fine, in_specs=in_specs, out_specs=out_specs, check_vma=False)
```

```python
import functools

import jax
import jax.numpy as jnp
from jax import lax
from jax.experimental import pallas as pl
from jax.experimental.pallas import tpu as pltpu
from jax.sharding import Mesh
from jax.sharding import PartitionSpec as P

HEAD_DIM = 64
SLOT = 8
TILE = 256
EPSILON = 1e-05
MASKED = -1e30
BF = jnp.bfloat16
F32 = jnp.float32

GROUP = ("core", "y")
CHIPS = ("z", "x", "y")
PLANE = ("z", "x")
EVEN = [(k * 4 + y, (1 - y // 2) * 4 + 2 * k + y % 2) for k in range(2) for y in range(4)]
ODD = [(k * 4 + y, (1 - y // 2) * 4 + 2 * k + 1 - y % 2) for k in range(2) for y in range(4)]
EVEN_BACK = [(b, a) for a, b in EVEN]
ODD_BACK = [(b, a) for a, b in ODD]


def dot(a, b, dims):
    return lax.dot_general(a, b, (dims, ((), ())), preferred_element_type=F32)


def nn(a, b):
    return dot(a, b, ((1,), (0,)))


def nt(a, b):
    return dot(a, b, ((1,), (1,)))


def tn(a, b):
    return dot(a, b, ((0,), (0,)))


def swap(value):
    return lax.ppermute(value, "core", [(0, 1), (1, 0)])


def ordered(first, one, two):
    return jnp.where(first, one, two), jnp.where(first, two, one)


def to_sequence(pair):
    return lax.ppermute(pair[0], GROUP, EVEN), lax.ppermute(pair[1], GROUP, ODD)


def scatter_sequence(half, even):
    low, high = half[:256], half[256:]
    mine, other = ordered(even, low, high)
    mine, other = lax.ppermute(mine, GROUP, EVEN_BACK), lax.ppermute(other, GROUP, ODD_BACK)
    return jnp.stack(ordered(even, mine, other))


def together(*values):
    return lax.optimization_barrier(values)


def standardize(values):
    centered = values - jnp.mean(values, -1, keepdims=True)
    inverse = lax.rsqrt(jnp.mean(centered * centered, -1, keepdims=True) + EPSILON)
    return centered * inverse, inverse


def norm_backward(upstream, standard, inverse, gain_vec):
    scaled = upstream * gain_vec
    return inverse * (
        scaled
        - jnp.mean(scaled, -1, keepdims=True)
        - standard * jnp.mean(scaled * standard, -1, keepdims=True)
    )


def sum_rows(values):
    return jnp.sum(values, 0, keepdims=True)


def call(kernel, grid, in_specs, out_specs, out_shape, scratch=(), vmem=28):
    return pl.pallas_call(
        kernel,
        grid=grid,
        in_specs=in_specs,
        out_specs=out_specs,
        out_shape=out_shape,
        scratch_shapes=scratch,
        compiler_params=pltpu.CompilerParams(vmem_limit_bytes=vmem * 2**20),
        cost_estimate=pl.CostEstimate(flops=100_000_000, bytes_accessed=2**16, transcendentals=0),
    )


WHOLE = pl.BlockSpec(memory_space=pltpu.VMEM)
SCALAR = pl.BlockSpec(memory_space=pltpu.SMEM)


def shape(dtype, *sizes):
    return jax.ShapeDtypeStruct(sizes, dtype)


def at_core(core, extent):
    return pl.ds(pl.multiple_of(core * extent, 128), extent)


def project_kernel(
    place_ref, own_a_ref, own_b_ref, other_a_ref, other_b_ref, weight_ref,
    normed_ref, mixed_ref, vector_ref, out_ref, token_ref,
):
    core, odd = place_ref[0], place_ref[1]
    row = lax.broadcasted_iota(jnp.int32, (8, 128), 0)
    col = lax.broadcasted_iota(jnp.int32, (8, 128), 1)
    vectors = nt((row == col).astype(BF), weight_ref[:, 1536:])
    vector_ref[...] = vectors
    out_ref[...] = weight_ref[:, 1152:1536]
    token_ref[at_core(odd, TILE), :] = own_a_ref[:, :768]
    token_ref[at_core(1 - odd, TILE), :] = own_b_ref[:, :768]
    pieces = ((1 - core, odd, own_a_ref), (1 - core, 1 - odd, own_b_ref))
    pieces += ((core, odd, other_a_ref), (core, 1 - odd, other_b_ref))
    for half, quarter, ref in pieces:
        standard, _ = standardize(ref[:, :768].astype(F32))
        normed = (standard * vectors[0:1] + vectors[1:2]).astype(BF)
        normed_ref[at_core(2 * half + quarter, TILE), :] = normed
    mixed_ref[...] = nn(normed_ref[...], weight_ref[:, :1152]).astype(BF)


def project(place, pieces, others, projections):
    return call(
        project_kernel,
        (),
        [SCALAR] + [WHOLE] * 5,
        [WHOLE] * 5,
        [
            shape(BF, 1024, 768),
            shape(BF, 1024, 1152),
            shape(F32, 8, 768),
            shape(BF, 768, 384),
            shape(BF, 512, 768),
        ],
        vmem=56,
    )(place, *pieces, *others, projections)


def leave_kernel(
    place_ref, own_ref, other_ref, mine_ref, theirs_ref, token_ref, vector_ref, slot_ref,
    middle_ref, attended_ref, sent_ref,
):
    core = place_ref[0]
    here, there = at_core(core, 384), at_core(1 - core, 384)
    attended_ref[:, here] = own_ref[...]
    attended_ref[:, there] = other_ref[...]
    middle_ref[:, here] = nn(attended_ref[...], mine_ref[...])
    middle_ref[:, there] = nn(attended_ref[...], theirs_ref[...])
    middle = token_ref[...].astype(F32) + middle_ref[...]
    middle_ref[...] = middle
    second = (standardize(middle)[0] * vector_ref[2:3, :] + vector_ref[3:4, :]).astype(BF)
    slots = lax.broadcasted_iota(jnp.int32, (1024, 512), 0) == slot_ref[...]
    sent_ref[...] = nn(slots.astype(BF), second).astype(BF)


def leave(place, own, other, mine, theirs, tokens, vectors, slots):
    return call(
        leave_kernel,
        (),
        [SCALAR] + [WHOLE] * 7,
        [WHOLE] * 3,
        [shape(F32, 512, 768), shape(BF, 512, 768), shape(BF, 1024, 768)],
    )(place, own, other, mine, theirs, tokens, vectors, slots.reshape(1, 512))


def enter_kernel(
    place_ref, back_ref, middle_ref, up_a_ref, up_b_ref, mine_ref, theirs_ref, vector_ref, slot_ref,
    grad_ref, low_ref, keep_ref, give_ref, sums_ref,
):
    core, odd = place_ref[0], place_ref[1]
    here, there = at_core(core, 384), at_core(1 - core, 384)
    grad_ref[at_core(odd, TILE), :] = up_a_ref[...].astype(F32)
    grad_ref[at_core(1 - odd, TILE), :] = up_b_ref[...].astype(F32)
    slots = lax.broadcasted_iota(jnp.int32, (1024, 512), 0) == slot_ref[...]
    second_grad = tn(slots.astype(BF), back_ref[...])
    standard, inverse = standardize(middle_ref[...])
    sums_ref[...] = jnp.zeros_like(sums_ref)
    sums_ref[2:3, :] = sum_rows(second_grad * standard)
    sums_ref[3:4, :] = sum_rows(second_grad)
    grad = grad_ref[...] + norm_backward(second_grad, standard, inverse, vector_ref[2:3, :])
    grad_ref[...] = grad
    low_ref[...] = grad.astype(BF)
    for ref, rows in ((keep_ref, here), (give_ref, there)):
        total = nt(low_ref[:, here], mine_ref[rows, :]) + nt(low_ref[:, there], theirs_ref[rows, :])
        ref[...] = total.astype(BF)


def enter(place, back_rows, middle, upstream, mine, theirs, vectors, slots):
    return call(
        enter_kernel,
        (),
        [SCALAR] + [WHOLE] * 8,
        [WHOLE] * 5,
        [
            shape(F32, 512, 768),
            shape(BF, 512, 768),
            shape(BF, 512, 384),
            shape(BF, 512, 384),
            shape(F32, 8, 768),
        ],
    )(place, back_rows, middle, *upstream, mine, theirs, vectors, slots.reshape(1, 512))


def share_kernel(normed_ref, mixed_ref, kept_ref, given_ref, share_ref):
    share_ref[:, :384] = tn(normed_ref[...], mixed_ref[...]).astype(BF)
    share_ref[:, 384:] = (kept_ref[...] + given_ref[...].astype(F32)).astype(BF)


def early_share(*values):
    return call(share_kernel, (), [WHOLE] * 4, WHOLE, shape(BF, 768, 768))(*values)


def finish_kernel(
    keep_ref, got_ref, token_ref, grad_ref, vector_ref, sums_ref, normed_ref, mixed_ref, out_ref, share_ref
):
    normed_grad = keep_ref[...] + got_ref[...].astype(F32)
    standard, inverse = standardize(token_ref[...].astype(F32))
    grad = grad_ref[...] + norm_backward(normed_grad, standard, inverse, vector_ref[0:1, :])
    out_ref[...] = grad.astype(BF)
    place = lax.broadcasted_iota(jnp.int32, (8, 768), 0)
    sums = jnp.where(place == 0, sum_rows(normed_grad * standard), sums_ref[...])
    sums = jnp.where(place == 1, sum_rows(normed_grad), sums)
    row = lax.broadcasted_iota(jnp.int32, (8, 128), 0)
    col = lax.broadcasted_iota(jnp.int32, (8, 128), 1)
    share_ref[:, 768:] = tn(sums.astype(BF), (row == col).astype(BF)).astype(BF)
    share_ref[:, :768] = tn(normed_ref[...], mixed_ref[...]).astype(BF)


def finish(*values):
    return call(
        finish_kernel,
        (),
        [WHOLE] * 8,
        [WHOLE] * 2,
        [shape(BF, 512, 768), shape(BF, 768, 896)],
        vmem=56,
    )(*values)


def head_lanes(head):
    lane = lax.broadcasted_iota(jnp.int32, (TILE, 128), 1)
    return lane < HEAD_DIM if head == 0 else lane >= HEAD_DIM


def one_head(value, head):
    return jnp.where(head_lanes(head), value, jnp.zeros_like(value))


def attend_forward_kernel(place_ref, q_ref, k_ref, v_ref, keep_ref, give_ref, log_ref):
    row = lax.broadcasted_iota(jnp.int32, (TILE, TILE), 0)
    col = lax.broadcasted_iota(jnp.int32, (TILE, TILE), 1)
    for i in range(q_ref.shape[0] // TILE):
        rows = pl.ds(i * TILE, TILE)
        queries = q_ref[rows, :] * jnp.asarray(HEAD_DIM**-0.5, BF)
        outs, logs = [], []
        for head in range(2):
            part = one_head(queries, head)
            scores = [nt(part, k_ref[pl.ds(j * TILE, TILE), :]) for j in range(i + 1)]
            scores[i] = jnp.where(col <= row, scores[i], MASKED)
            top = functools.reduce(jnp.maximum, [jnp.max(s, axis=1, keepdims=True) for s in scores])
            weights = [jnp.exp(s - top) for s in scores]
            total = functools.reduce(jnp.add, [jnp.sum(w, axis=1, keepdims=True) for w in weights])
            out = functools.reduce(
                jnp.add, [nn(weights[j].astype(BF), v_ref[pl.ds(j * TILE, TILE), :]) for j in range(i + 1)]
            )
            outs.append(out * (1.0 / total))
            logs.append(jnp.broadcast_to(top + jnp.log(total), (TILE, 128)))
        out = jnp.where(head_lanes(0), outs[0], outs[1]).astype(BF)
        within, ours = pl.ds(i % 2 * TILE, TILE), place_ref[0] == 1 - i // 2

        @pl.when(ours)
        def _():
            keep_ref[within, :] = out

        @pl.when(jnp.logical_not(ours))
        def _():
            give_ref[within, :] = out

        log_ref[rows, :] = jnp.where(head_lanes(0), logs[0], logs[1])


def attend_forward(place, mixed):
    length, width = mixed.shape
    pairs = width // 384

    def at(shift, rows=length):
        return pl.BlockSpec((rows, 128), lambda p: (0, p + shift))

    return call(
        attend_forward_kernel,
        (pairs,),
        [SCALAR, at(0), at(pairs), at(2 * pairs)],
        [at(0, 512), at(0, 512), at(0)],
        [shape(BF, 512, 128 * pairs), shape(BF, 512, 128 * pairs), shape(F32, length, 128 * pairs)],
        vmem=56,
    )(place, mixed, mixed, mixed)


def attend_backward_kernel(
    place_ref, q_ref, k_ref, v_ref, own_o_ref, other_o_ref, own_g_ref, other_g_ref, log_ref, *refs
):
    *others, k_sum, v_sum = refs
    out_ref = others[0] if len(others) == 1 else others[2]

    def columns(part):
        start = part * (out_ref.shape[1] // 3) + pl.program_id(0) * 128
        return pl.ds(pl.multiple_of(start, 128), 128)

    key = lax.broadcasted_iota(jnp.int32, (TILE, TILE), 0)
    query = lax.broadcasted_iota(jnp.int32, (TILE, TILE), 1)
    k_sum[...] = jnp.zeros_like(k_sum)
    v_sum[...] = jnp.zeros_like(v_sum)
    for i in range(q_ref.shape[0] // TILE):
        rows = pl.ds(i * TILE, TILE)
        queries = q_ref[rows, :] * jnp.asarray(HEAD_DIM**-0.5, BF)
        within, ours = pl.ds(i % 2 * TILE, TILE), place_ref[0] == 1 - i // 2
        up = jnp.where(ours, own_g_ref[within, :], other_g_ref[within, :])
        heads = jnp.where(ours, own_o_ref[within, :], other_o_ref[within, :])
        product = (up.astype(F32) * heads.astype(F32)).T
        logs = log_ref[rows, :].T
        sums = []
        for head in range(2):
            q_part, g_part = one_head(queries, head), one_head(up, head)
            row_dot = jnp.sum(product[64 * head : 64 * head + 64], axis=0, keepdims=True)
            log_row = logs[64 * head : 64 * head + 1]
            total = None
            for j in range(i + 1):
                cols = pl.ds(j * TILE, TILE)
                scores = nt(k_ref[cols, :], q_part)
                if j == i:
                    scores = jnp.where(key <= query, scores, MASKED)
                probs = jnp.exp(scores - log_row)
                prob_grad = nt(v_ref[cols, :], g_part)
                score_grad = (probs * (prob_grad - row_dot)).astype(BF)
                v_sum[cols, :] += nn(probs.astype(BF), g_part)
                k_sum[cols, :] += nn(score_grad, q_part)
                term = tn(score_grad, k_ref[cols, :])
                total = term if total is None else total + term
            sums.append(total)
        grad = jnp.where(head_lanes(0), sums[0], sums[1]) * HEAD_DIM**-0.5
        out_ref[rows, columns(0)] = grad.astype(BF)
    out_ref[:, columns(1)] = k_sum[...].astype(BF)
    out_ref[:, columns(2)] = v_sum[...].astype(BF)

    if len(others) > 1:
        weight_ref, before_ref, _, keep_ref, give_ref = others

        @pl.when(pl.program_id(0) == pl.num_programs(0) - 1)
        def _():
            core = place_ref[0]
            for half, ref in ((1 - core, keep_ref), (core, give_ref)):
                rows, total = at_core(half, 512), None
                for source, first in ((before_ref, 0), (out_ref, 128)):
                    width = source.shape[1] // 3
                    for part in range(3):
                        weight = weight_ref[:, 384 * part + first : 384 * part + first + width]
                        term = nt(source[rows, width * part : width * part + width], weight)
                        total = term if total is None else total + term
                ref[...] = total.astype(ref.dtype)


def attend_backward(place, mixed, heads, grads, logs, first, count, *more):
    length, width = mixed.shape
    pairs = width // 384

    def at(shift, rows=length):
        return pl.BlockSpec((rows, 128), lambda p: (0, p + shift + first))

    def whole(*sizes):
        return pl.BlockSpec(sizes, lambda p: (0, 0))

    out, out_specs = [shape(BF, length, 384 * count)], [whole(length, 384 * count)]
    if more:
        out += [shape(F32, 512, 768), shape(BF, 512, 768)]
        out_specs += [whole(512, 768)] * 2
    return call(
        attend_backward_kernel,
        (count,),
        [SCALAR, at(0), at(pairs), at(2 * pairs)]
        + [at(0, 512)] * 4
        + [at(0)]
        + [whole(*item.shape) for item in more],
        out_specs,
        out,
        [pltpu.VMEM((length, 128), F32)] * 2,
        vmem=56,
    )(place, mixed, mixed, mixed, *heads, *grads, logs, *more)


def of_block(which):
    return pl.BlockSpec((1, 768, 768), lambda i: (which, 0, 0))


def rows_of(count, width):
    return pl.BlockSpec((count, width), lambda i: (i, 0))


def act_grad_kernel(place_ref, own_ref, other_ref, *refs):
    core = place_ref[0]
    out_ref, aligned_ref, held = refs[4:]
    for group in range(4):
        for ref, at in ((own_ref, core), (other_ref, 1 - core)):
            rows = pl.ds(pl.multiple_of(64 * group + 32 * at, 32), 32)
            held[rows, :] = ref[pl.ds(pl.multiple_of(64 * group + 32 * (1 - core), 32), 32), :]
    row = lax.broadcasted_iota(jnp.int32, (TILE, TILE), 0)
    col = lax.broadcasted_iota(jnp.int32, (TILE, TILE), 1)
    taken = row // 32 * 32 + row % 8 + row // 8 % 2 * 16 + row // 16 % 2 * 8
    aligned_ref[...] = nn((taken == col).astype(BF), held[...]).astype(BF)
    for i, block in enumerate(refs[:4]):
        out_ref[:, 768 * i : 768 * i + 768] = nt(aligned_ref[...], block[0]).astype(BF)


def act_grads(place, own, other, blocks):
    count = own.shape[0]
    return call(
        act_grad_kernel,
        (4,),
        [SCALAR] + [rows_of(count // 4, 768)] * 2 + [of_block(1)] * 4,
        [rows_of(count // 4, 3072), rows_of(count // 4, 768)],
        [shape(BF, count, 3072), shape(BF, count, 768)],
        [pltpu.VMEM((count // 4, 768), BF)],
        vmem=56,
    )(place, own, other, *blocks)


def expert_kernel(row_ref, grad_ref, *refs):
    act_ref, pre_ref, out_ref = refs[4:]
    rows = row_ref[...]
    total = None
    for i, block in enumerate(refs[:4]):
        cols = slice(768 * i, 768 * i + 768)
        weight = block[0]
        pre = nn(rows, weight)
        cumulative = 0.5 * (1.0 + lax.erf(pre * 0.7071067811865476))
        act_ref[:, cols] = (pre * cumulative).astype(BF)
        slope = cumulative + pre * jnp.exp(-0.5 * pre * pre) * 0.3989422804014327
        grad = (grad_ref[:, cols].astype(F32) * slope).astype(BF)
        pre_ref[:, cols] = grad
        term = nt(grad, weight)
        total = term if total is None else total + term
    out_ref[...] = total.astype(BF)


def expert(rows, act_grad, blocks):
    count = rows.shape[0]
    wide = jax.ShapeDtypeStruct((count, 3072), BF)
    return call(
        expert_kernel,
        (4,),
        [rows_of(count // 4, 768), rows_of(count // 4, 3072)] + [of_block(0)] * 4,
        [rows_of(count // 4, 3072), rows_of(count // 4, 3072), rows_of(count // 4, 768)],
        [wide, wide, jax.ShapeDtypeStruct((count, 768), BF)],
        vmem=56,
    )(rows, act_grad, *blocks)


def result_kernel(act_ref, *refs):
    terms = [nn(act_ref[:, 768 * i : 768 * i + 768], refs[i][0]) for i in range(4)]
    refs[4][...] = functools.reduce(jnp.add, terms).astype(BF)


def expert_results(activated, blocks):
    count = activated.shape[0]
    return call(
        result_kernel,
        (4,),
        [rows_of(count // 4, 3072)] + [of_block(1)] * 4,
        rows_of(count // 4, 768),
        jax.ShapeDtypeStruct((count, 768), BF),
        vmem=56,
    )(activated, *blocks)


def weight_grad_kernel(row_ref, grad_ref, act_ref, pre_ref, *refs):
    one, two = tn(row_ref[...], pre_ref[...]), tn(act_ref[...], grad_ref[...])
    if len(refs) == 1:
        refs[0][0, 0] = one.astype(BF)
        refs[0][0, 1] = two.astype(BF)
        return
    one, two = one + refs[0][0, 0].astype(F32), two + refs[0][0, 1].astype(F32)
    for step, ref in enumerate(refs[1:]):

        @pl.when(pl.program_id(0) == step)
        def _():
            ref[0] = one.astype(BF)
            ref[1] = two.astype(BF)


def weight_grads(rows, grads, activated, pre_grad, start, *others):
    count = rows.shape[0]
    whole = pl.BlockSpec((count, 768), lambda i: (0, 0))
    block = pl.BlockSpec((count, 768), lambda i: (0, i + start))
    both = pl.BlockSpec((1, 2, 768, 768), lambda i: (i, 0, 0, 0))
    single = pl.BlockSpec((2, 768, 768), lambda i: (0, 0, 0))
    return call(
        weight_grad_kernel,
        (2,),
        [whole, whole, block, block] + [both] * len(others),
        [single, single] if others else both,
        [shape(BF, 2, 768, 768)] * 2 if others else shape(BF, 2, 2, 768, 768),
        vmem=56,
    )(rows, grads, activated, pre_grad, *others)


def place_kernel(even_ref, a_ref, b_ref, in_ref, out_ref):
    from_a = (pl.program_id(1) == 0) == (even_ref[0] == 1)

    @pl.when(from_a)
    def _():
        in_ref[0] = a_ref[0].astype(F32)
        out_ref[0] = a_ref[1].astype(F32)

    @pl.when(jnp.logical_not(from_a))
    def _():
        in_ref[0] = b_ref[0].astype(F32)
        out_ref[0] = b_ref[1].astype(F32)


def place_expert_grads(even, grad_a, grad_b):
    taken = pl.BlockSpec((2, 256, 768), lambda i, e: (0, i, 0))
    given = pl.BlockSpec((1, 256, 768), lambda i, e: (e, i, 0))
    return call(
        place_kernel,
        (3, 2),
        [pl.BlockSpec(memory_space=pltpu.SMEM), taken, taken],
        [given, given],
        [jax.ShapeDtypeStruct((2, 768, 768), F32)] * 2,
    )(even.astype(jnp.int32).reshape(1), grad_a, grad_b)


def slots_of(ids):
    blocks = ids.reshape(2, 256)
    same = blocks[:, :, None] == blocks[:, None, :]
    places = jnp.arange(256, dtype=jnp.int32)
    rank = jnp.sum((same & (places[None, :] < places[:, None])).astype(jnp.int32), -1)
    slots = blocks * (2 * SLOT) + jnp.arange(2, dtype=jnp.int32)[:, None] * SLOT + rank
    return slots.reshape(512)


def slot_rows(rows, slots):
    matrix = jnp.arange(1024, dtype=jnp.int32)[:, None] == slots[None, :]
    return nn(matrix.astype(BF), rows).astype(BF)


def token_rows(rows, slots):
    matrix = slots[:, None] == jnp.arange(1024, dtype=jnp.int32)[None, :]
    return nn(matrix.astype(BF), rows)


def exchange(rows):
    return lax.all_to_all(rows.reshape(64, 16, -1), CHIPS, 0, 0, tiled=True).reshape(1024, -1)


def halve_kernel(qkv_ref, out_ref, vector_ref, halves_ref):
    row = lax.broadcasted_iota(jnp.int32, (4, 128), 0)
    col = lax.broadcasted_iota(jnp.int32, (4, 128), 1)
    columns = tn(vector_ref[...], (row == col).astype(BF)).astype(BF)
    for core in range(2):
        cuts = [qkv_ref[:, 768 * i + 384 * core : 768 * i + 384 * core + 384] for i in range(3)]
        half = jnp.concatenate(cuts + [out_ref[:, 384 * core : 384 * core + 384], columns], 1)
        for chip in range(4):
            halves_ref[4 * core + chip] = half


def gather_group(qkv, out, vectors):
    sent = call(halve_kernel, (), [WHOLE] * 3, WHOLE, shape(BF, 8, 6, 1664))(qkv, out, jnp.stack(vectors))
    return lax.all_to_all(sent, GROUP, 0, 0, tiled=True).reshape(1, 48, 1664)


def reduce_plane(grads):
    got = lax.all_to_all(grads.reshape(16, 48, -1), PLANE, 0, 0, tiled=True)
    return jnp.sum(got.astype(F32), 0)


def reduce_projections(rows, first):
    rows = rows.reshape(2, 4, 6, 1664)
    place = lax.axis_index("y")

    def part(of):
        return lax.dynamic_slice_in_dim(rows, of % 4, 1, 1).reshape(2, 6, 1664)

    total = part(place)
    for shift in (2, 1, 3):
        total = total + lax.ppermute(part(place + shift), "y", [(i, (i + shift) % 4) for i in range(4)])
    keep, give = ordered(first, total[0], total[1])
    both = ordered(first, keep, swap(give))
    qkv = jnp.stack([half[:, :1152].reshape(6, 3, 384) for half in both], 2).reshape(6, 2304)
    out = jnp.concatenate([half[:, 1152:1536] for half in both], 1)
    return qkv, out, both[0][:, 1536:1540] + both[1][:, 1536:1540]


def local(
    tokens,
    buckets,
    qkv_weight,
    output_weight,
    attend_gain,
    attend_bias,
    expert_gain,
    expert_bias,
    expert_in,
    expert_out,
    cotangent,
):
    even = lax.axis_index("y") % 2 == 0
    first = lax.axis_index("core") == 0
    place = jnp.stack((lax.axis_index("core"), lax.axis_index("y") % 2)).astype(jnp.int32)

    def halves(value, extent, axis=0):
        return ordered(
            first,
            lax.slice_in_dim(value, 0, extent, axis=axis),
            lax.slice_in_dim(value, extent, 2 * extent, axis=axis),
        )

    rows = gather_group(qkv_weight, output_weight, (attend_gain, attend_bias, expert_gain, expert_bias))
    packed = jnp.pad(buckets.astype(BF), ((0, 0), (0, 0), (0, 127)))
    packed = jnp.concatenate((tokens, packed), -1)
    packed = ordered(even, packed[0], packed[1])
    experts = jnp.stack((expert_in, expert_out), 1)
    experts = ordered(even, experts[0], experts[1])
    rows, *moving = together(rows, *packed, *experts)
    pieces = to_sequence(moving[:2])
    block_a, block_b = to_sequence(moving[2:])
    sent = jnp.broadcast_to(rows, (16, 48, 1664))
    projections = lax.all_to_all(sent, PLANE, 0, 0, tiled=True).reshape(768, 1664)

    grad_slots = slot_rows(cotangent.reshape(512, 768), slots_of(buckets.reshape(512)))
    slots = jnp.concatenate(ordered(even, pieces[0][:, 768], pieces[1][:, 768]))
    slots = slots_of(slots.astype(jnp.int32))
    grad_rows = exchange(grad_slots)

    others = [swap(piece) for piece in pieces]
    normed, mixed, vectors, out_mine, token_half = project(place, pieces, others, projections)
    out_theirs = swap(out_mine)
    *heads, logs = attend_forward(place, mixed)
    middle, attended, sent = leave(
        place, heads[0], swap(heads[1]), out_mine, out_theirs, token_half, vectors, slots
    )
    sent, block_a, block_b, grad_rows = together(sent, block_a, block_b, grad_rows)
    blocks = (block_a, block_b, swap(block_a), swap(block_b))
    rows = exchange(sent)
    act_grad, grad_rows = act_grads(place, grad_rows, swap(grad_rows), blocks)
    act_grad, *upstream = together(act_grad, *ordered(even, cotangent[0], cotangent[1]))
    upstream = to_sequence(upstream)
    activated, pre_grad, row_grad = expert(rows, act_grad, blocks)
    row_grad, *upstream = together(row_grad, *upstream)
    back_rows = exchange(row_grad)
    result = expert_results(activated, blocks)
    result, pre_grad = together(result, pre_grad)
    made = (rows, grad_rows, activated, pre_grad)
    theirs = weight_grads(*made, 2)
    back_rows, theirs, result = together(back_rows, theirs, result)
    result_rows = exchange(result)
    grad_a, grad_b = weight_grads(*made, 0, swap(theirs))
    back_rows, grad_a, grad_b = together(back_rows, grad_a, grad_b)
    grad_a, grad_b = lax.ppermute(grad_a, GROUP, EVEN_BACK), lax.ppermute(grad_b, GROUP, ODD_BACK)

    middle_grad, branch_grad, keep, give, sums = enter(
        place, back_rows, middle, upstream, out_mine, out_theirs, vectors, slots
    )
    keep, got, result_rows = together(keep, swap(give), result_rows)
    (early_grad,) = attend_backward(place, mixed, heads, (keep, got), logs, 0, 1)
    out_keep, out_give = halves(tn(attended, branch_grad), 384, 1)
    early = early_share(normed, early_grad, out_keep, swap(out_give.astype(BF)))
    early, mixed = together(early, mixed)
    early = reduce_plane(early)
    late_grad, keep, give = attend_backward(
        place, mixed, heads, (keep, got), logs, 1, 2, projections, early_grad
    )
    token_grad, late = finish(keep, swap(give), token_half, middle_grad, vectors, sums, normed, late_grad)
    late, grad_a, grad_b = together(late, grad_a, grad_b)
    token_grad = scatter_sequence(token_grad, even)
    block_out = scatter_sequence((middle + token_rows(result_rows, slots)).astype(BF), even)
    expert_in_grad, expert_out_grad = place_expert_grads(even, grad_a, grad_b)
    late = reduce_plane(late)
    cuts = []
    for i in range(3):
        cuts += [early[:, 128 * i : 128 * i + 128], late[:, 256 * i : 256 * i + 256]]
    summed = jnp.concatenate(cuts + [early[:, 384:], late[:, 768:]], 1)
    summed, expert_in_grad, expert_out_grad = together(summed, expert_in_grad, expert_out_grad)
    qkv_grad, outproj_grad, shares = reduce_projections(summed, first)
    return (
        block_out,
        token_grad,
        qkv_grad,
        outproj_grad,
        shares[:, 0],
        shares[:, 1],
        shares[:, 2],
        shares[:, 3],
        expert_in_grad,
        expert_out_grad,
    )


def solution(mesh):
    fine = Mesh(mesh.devices.reshape(4, 4, 2, 4), ("z", "x", "core", "y"))
    dp, every = ("z", "x", "core"), ("z", "x", "core", "y")
    rows = P(dp, "y", None)
    in_specs = (
        rows,
        rows,
        P(every, None),
        P(every, None),
        P(every),
        P(every),
        P(every),
        P(every),
        P(dp, None, "y"),
        P(dp, "y", None),
        rows,
    )
    out_specs = (
        rows,
        rows,
        P(every, None),
        P(every, None),
        P(every),
        P(every),
        P(every),
        P(every),
        P(dp, None, "y"),
        P(dp, "y", None),
    )
    return jax.shard_map(local, mesh=fine, in_specs=in_specs, out_specs=out_specs, check_vma=False)
```

```python
import functools

import jax
import jax.numpy as jnp
from jax import lax
from jax.experimental import pallas as pl
from jax.experimental.pallas import tpu as pltpu
from jax.sharding import Mesh
from jax.sharding import PartitionSpec as P

HEAD_DIM = 64
SLOT = 8
TILE = 256
EPSILON = 1e-05
MASKED = -1e30
BF = jnp.bfloat16
F32 = jnp.float32

GROUP = ("core", "y")
CHIPS = ("z", "x", "y")
PLANE = ("z", "x")
EVEN = [(k * 4 + y, (1 - y // 2) * 4 + 2 * k + y % 2) for k in range(2) for y in range(4)]
ODD = [(k * 4 + y, (1 - y // 2) * 4 + 2 * k + 1 - y % 2) for k in range(2) for y in range(4)]
EVEN_BACK = [(b, a) for a, b in EVEN]
ODD_BACK = [(b, a) for a, b in ODD]


def dot(a, b, dims):
    return lax.dot_general(a, b, (dims, ((), ())), preferred_element_type=F32)


def nn(a, b):
    return dot(a, b, ((1,), (0,)))


def nt(a, b):
    return dot(a, b, ((1,), (1,)))


def tn(a, b):
    return dot(a, b, ((0,), (0,)))


def swap(value):
    return lax.ppermute(value, "core", [(0, 1), (1, 0)])


def ordered(first, one, two):
    return jnp.where(first, one, two), jnp.where(first, two, one)


def to_sequence(pair):
    return lax.ppermute(pair[0], GROUP, EVEN), lax.ppermute(pair[1], GROUP, ODD)


def scatter_sequence(half, even):
    low, high = half[:256], half[256:]
    mine, other = ordered(even, low, high)
    mine, other = lax.ppermute(mine, GROUP, EVEN_BACK), lax.ppermute(other, GROUP, ODD_BACK)
    return jnp.stack(ordered(even, mine, other))


def together(*values):
    return lax.optimization_barrier(values)


def standardize(values):
    centered = values - jnp.mean(values, -1, keepdims=True)
    inverse = lax.rsqrt(jnp.mean(centered * centered, -1, keepdims=True) + EPSILON)
    return centered * inverse, inverse


def norm_backward(upstream, standard, inverse, gain_vec):
    scaled = upstream * gain_vec
    return inverse * (
        scaled
        - jnp.mean(scaled, -1, keepdims=True)
        - standard * jnp.mean(scaled * standard, -1, keepdims=True)
    )


def sum_rows(values):
    return jnp.sum(values, 0, keepdims=True)


def call(kernel, grid, in_specs, out_specs, out_shape, scratch=(), vmem=28):
    return pl.pallas_call(
        kernel,
        grid=grid,
        in_specs=in_specs,
        out_specs=out_specs,
        out_shape=out_shape,
        scratch_shapes=scratch,
        compiler_params=pltpu.CompilerParams(vmem_limit_bytes=vmem * 2**20),
        cost_estimate=pl.CostEstimate(flops=100_000_000, bytes_accessed=2**16, transcendentals=0),
    )


WHOLE = pl.BlockSpec(memory_space=pltpu.VMEM)
SCALAR = pl.BlockSpec(memory_space=pltpu.SMEM)


def shape(dtype, *sizes):
    return jax.ShapeDtypeStruct(sizes, dtype)


def at_core(core, extent):
    return pl.ds(pl.multiple_of(core * extent, 128), extent)


def project_kernel(
    place_ref, own_a_ref, own_b_ref, other_a_ref, other_b_ref, weight_ref,
    normed_ref, mixed_ref, vector_ref, out_ref, token_ref,
):
    core, odd = place_ref[0], place_ref[1]
    row = lax.broadcasted_iota(jnp.int32, (8, 128), 0)
    col = lax.broadcasted_iota(jnp.int32, (8, 128), 1)
    vectors = nt((row == col).astype(BF), weight_ref[:, 1536:])
    vector_ref[...] = vectors
    out_ref[...] = weight_ref[:, 1152:1536]
    token_ref[at_core(odd, TILE), :] = own_a_ref[:, :768]
    token_ref[at_core(1 - odd, TILE), :] = own_b_ref[:, :768]
    pieces = ((1 - core, odd, own_a_ref), (1 - core, 1 - odd, own_b_ref))
    pieces += ((core, odd, other_a_ref), (core, 1 - odd, other_b_ref))
    for half, quarter, ref in pieces:
        standard, _ = standardize(ref[:, :768].astype(F32))
        normed = (standard * vectors[0:1] + vectors[1:2]).astype(BF)
        normed_ref[at_core(2 * half + quarter, TILE), :] = normed
    mixed_ref[...] = nn(normed_ref[...], weight_ref[:, :1152]).astype(BF)


def project(place, pieces, others, projections):
    return call(
        project_kernel,
        (),
        [SCALAR] + [WHOLE] * 5,
        [WHOLE] * 5,
        [
            shape(BF, 1024, 768),
            shape(BF, 1024, 1152),
            shape(F32, 8, 768),
            shape(BF, 768, 384),
            shape(BF, 512, 768),
        ],
        vmem=56,
    )(place, *pieces, *others, projections)


def leave_kernel(
    place_ref, own_ref, other_ref, mine_ref, theirs_ref, token_ref, vector_ref, slot_ref,
    middle_ref, attended_ref, sent_ref,
):
    core = place_ref[0]
    here, there = at_core(core, 384), at_core(1 - core, 384)
    attended_ref[:, here] = own_ref[...]
    attended_ref[:, there] = other_ref[...]
    middle_ref[:, here] = nn(attended_ref[...], mine_ref[...])
    middle_ref[:, there] = nn(attended_ref[...], theirs_ref[...])
    middle = token_ref[...].astype(F32) + middle_ref[...]
    middle_ref[...] = middle
    second = (standardize(middle)[0] * vector_ref[2:3, :] + vector_ref[3:4, :]).astype(BF)
    slots = lax.broadcasted_iota(jnp.int32, (1024, 512), 0) == slot_ref[...]
    sent_ref[...] = nn(slots.astype(BF), second).astype(BF)


def leave(place, own, other, mine, theirs, tokens, vectors, slots):
    return call(
        leave_kernel,
        (),
        [SCALAR] + [WHOLE] * 7,
        [WHOLE] * 3,
        [shape(F32, 512, 768), shape(BF, 512, 768), shape(BF, 1024, 768)],
    )(place, own, other, mine, theirs, tokens, vectors, slots.reshape(1, 512))


def enter_kernel(
    place_ref, back_ref, middle_ref, up_a_ref, up_b_ref, mine_ref, theirs_ref, vector_ref, slot_ref,
    grad_ref, low_ref, keep_ref, give_ref, sums_ref,
):
    core, odd = place_ref[0], place_ref[1]
    here, there = at_core(core, 384), at_core(1 - core, 384)
    grad_ref[at_core(odd, TILE), :] = up_a_ref[...].astype(F32)
    grad_ref[at_core(1 - odd, TILE), :] = up_b_ref[...].astype(F32)
    slots = lax.broadcasted_iota(jnp.int32, (1024, 512), 0) == slot_ref[...]
    second_grad = tn(slots.astype(BF), back_ref[...])
    standard, inverse = standardize(middle_ref[...])
    sums_ref[...] = jnp.zeros_like(sums_ref)
    sums_ref[2:3, :] = sum_rows(second_grad * standard)
    sums_ref[3:4, :] = sum_rows(second_grad)
    grad = grad_ref[...] + norm_backward(second_grad, standard, inverse, vector_ref[2:3, :])
    grad_ref[...] = grad
    low_ref[...] = grad.astype(BF)
    for ref, rows in ((keep_ref, here), (give_ref, there)):
        total = nt(low_ref[:, here], mine_ref[rows, :]) + nt(low_ref[:, there], theirs_ref[rows, :])
        ref[...] = total.astype(BF)


def enter(place, back_rows, middle, upstream, mine, theirs, vectors, slots):
    return call(
        enter_kernel,
        (),
        [SCALAR] + [WHOLE] * 8,
        [WHOLE] * 5,
        [
            shape(F32, 512, 768),
            shape(BF, 512, 768),
            shape(BF, 512, 384),
            shape(BF, 512, 384),
            shape(F32, 8, 768),
        ],
    )(place, back_rows, middle, *upstream, mine, theirs, vectors, slots.reshape(1, 512))


def share_kernel(normed_ref, mixed_ref, kept_ref, given_ref, share_ref):
    share_ref[:, :384] = tn(normed_ref[...], mixed_ref[...]).astype(BF)
    share_ref[:, 384:] = (kept_ref[...] + given_ref[...].astype(F32)).astype(BF)


def early_share(*values):
    return call(share_kernel, (), [WHOLE] * 4, WHOLE, shape(BF, 768, 768))(*values)


def finish_kernel(
    keep_ref, got_ref, token_ref, grad_ref, vector_ref, sums_ref, normed_ref, mixed_ref, out_ref, share_ref
):
    normed_grad = keep_ref[...] + got_ref[...].astype(F32)
    standard, inverse = standardize(token_ref[...].astype(F32))
    grad = grad_ref[...] + norm_backward(normed_grad, standard, inverse, vector_ref[0:1, :])
    out_ref[...] = grad.astype(BF)
    place = lax.broadcasted_iota(jnp.int32, (8, 768), 0)
    sums = jnp.where(place == 0, sum_rows(normed_grad * standard), sums_ref[...])
    sums = jnp.where(place == 1, sum_rows(normed_grad), sums)
    row = lax.broadcasted_iota(jnp.int32, (8, 128), 0)
    col = lax.broadcasted_iota(jnp.int32, (8, 128), 1)
    share_ref[:, 768:] = tn(sums.astype(BF), (row == col).astype(BF)).astype(BF)
    share_ref[:, :768] = tn(normed_ref[...], mixed_ref[...]).astype(BF)


def finish(*values):
    return call(
        finish_kernel,
        (),
        [WHOLE] * 8,
        [WHOLE] * 2,
        [shape(BF, 512, 768), shape(BF, 768, 896)],
    )(*values)


def head_lanes(head):
    lane = lax.broadcasted_iota(jnp.int32, (TILE, 128), 1)
    return lane < HEAD_DIM if head == 0 else lane >= HEAD_DIM


def both_heads(value):
    parts = [jnp.where(head_lanes(head), value, jnp.zeros_like(value)) for head in range(2)]
    return jnp.concatenate(parts, 0)


def side_by_side(value):
    return jnp.where(head_lanes(0), value[:TILE], value[TILE:])


def attend_forward_kernel(place_ref, q_ref, k_ref, v_ref, keep_ref, give_ref, log_ref):
    row = lax.broadcasted_iota(jnp.int32, (2 * TILE, TILE), 0)
    allowed = lax.broadcasted_iota(jnp.int32, (2 * TILE, TILE), 1) <= lax.rem(row, TILE)
    for i in range(q_ref.shape[0] // TILE):
        rows = pl.ds(i * TILE, TILE)
        queries = both_heads(q_ref[rows, :] * jnp.asarray(HEAD_DIM**-0.5, BF))
        tiles = [pl.ds(j * TILE, TILE) for j in range(i + 1)]
        scores = [nt(queries, k_ref[tile, :]) for tile in tiles]
        scores[i] = jnp.where(allowed, scores[i], MASKED)
        top = functools.reduce(jnp.maximum, [jnp.max(s, axis=1, keepdims=True) for s in scores])
        weights = [jnp.exp(s - top) for s in scores]
        total = functools.reduce(jnp.add, [jnp.sum(w, axis=1, keepdims=True) for w in weights])
        terms = [nn(w.astype(BF), v_ref[tile, :]) for w, tile in zip(weights, tiles)]
        out = side_by_side(functools.reduce(jnp.add, terms) * (1.0 / total)).astype(BF)
        within, ours = pl.ds(i % 2 * TILE, TILE), place_ref[0] == 1 - i // 2

        @pl.when(ours)
        def _():
            keep_ref[within, :] = out

        @pl.when(jnp.logical_not(ours))
        def _():
            give_ref[within, :] = out

        log_ref[rows, :] = side_by_side(jnp.broadcast_to(top + jnp.log(total), (2 * TILE, 128)))


def attend_forward(place, mixed):
    length, width = mixed.shape
    pairs = width // 384

    def at(shift, rows=length):
        return pl.BlockSpec((rows, 128), lambda p: (0, p + shift))

    return call(
        attend_forward_kernel,
        (pairs,),
        [SCALAR, at(0), at(pairs), at(2 * pairs)],
        [at(0, 512), at(0, 512), at(0)],
        [shape(BF, 512, 128 * pairs), shape(BF, 512, 128 * pairs), shape(F32, length, 128 * pairs)],
        vmem=56,
    )(place, mixed, mixed, mixed)


def attend_backward_kernel(
    place_ref, q_ref, k_ref, v_ref, own_o_ref, other_o_ref, own_g_ref, other_g_ref, log_ref, *refs
):
    *others, k_sum, v_sum = refs
    out_ref = others[0] if len(others) == 1 else others[2]

    def columns(part):
        start = part * (out_ref.shape[1] // 3) + pl.program_id(0) * 128
        return pl.ds(pl.multiple_of(start, 128), 128)

    query = lax.broadcasted_iota(jnp.int32, (TILE, 2 * TILE), 1)
    allowed = lax.broadcasted_iota(jnp.int32, (TILE, 2 * TILE), 0) <= lax.rem(query, TILE)
    k_sum[...] = jnp.zeros_like(k_sum)
    v_sum[...] = jnp.zeros_like(v_sum)
    for i in range(q_ref.shape[0] // TILE):
        rows = pl.ds(i * TILE, TILE)
        within, ours = pl.ds(i % 2 * TILE, TILE), place_ref[0] == 1 - i // 2
        up = jnp.where(ours, own_g_ref[within, :], other_g_ref[within, :])
        heads = jnp.where(ours, own_o_ref[within, :], other_o_ref[within, :])
        product = (up.astype(F32) * heads.astype(F32)).T
        logs = log_ref[rows, :].T
        queries = both_heads(q_ref[rows, :] * jnp.asarray(HEAD_DIM**-0.5, BF))
        grads = both_heads(up)
        row_dots = [jnp.sum(product[64 * head : 64 * head + 64], axis=0, keepdims=True) for head in range(2)]
        row_dots = jnp.concatenate(row_dots, 1)
        log_row = jnp.concatenate([logs[0:1], logs[64:65]], 1)
        total = None
        for j in range(i + 1):
            cols = pl.ds(j * TILE, TILE)
            scores = nt(k_ref[cols, :], queries)
            if j == i:
                scores = jnp.where(allowed, scores, MASKED)
            probs = jnp.exp(scores - log_row)
            prob_grad = nt(v_ref[cols, :], grads)
            score_grad = (probs * (prob_grad - row_dots)).astype(BF)
            v_sum[cols, :] += nn(probs.astype(BF), grads)
            k_sum[cols, :] += nn(score_grad, queries)
            term = tn(score_grad, k_ref[cols, :])
            total = term if total is None else total + term
        out_ref[rows, columns(0)] = (side_by_side(total) * HEAD_DIM**-0.5).astype(BF)
    out_ref[:, columns(1)] = k_sum[...].astype(BF)
    out_ref[:, columns(2)] = v_sum[...].astype(BF)

    if len(others) > 1:
        weight_ref, before_ref, _, keep_ref, give_ref = others

        @pl.when(pl.program_id(0) == pl.num_programs(0) - 1)
        def _():
            core = place_ref[0]
            for half, ref in ((1 - core, keep_ref), (core, give_ref)):
                rows, total = at_core(half, 512), None
                for source, first in ((before_ref, 0), (out_ref, 128)):
                    width = source.shape[1] // 3
                    for part in range(3):
                        weight = weight_ref[:, 384 * part + first : 384 * part + first + width]
                        term = nt(source[rows, width * part : width * part + width], weight)
                        total = term if total is None else total + term
                ref[...] = total.astype(ref.dtype)


def attend_backward(place, mixed, heads, grads, logs, first, count, *more):
    length, width = mixed.shape
    pairs = width // 384

    def at(shift, rows=length):
        return pl.BlockSpec((rows, 128), lambda p: (0, p + shift + first))

    def whole(*sizes):
        return pl.BlockSpec(sizes, lambda p: (0, 0))

    out, out_specs = [shape(BF, length, 384 * count)], [whole(length, 384 * count)]
    if more:
        out += [shape(F32, 512, 768), shape(BF, 512, 768)]
        out_specs += [whole(512, 768)] * 2
    return call(
        attend_backward_kernel,
        (count,),
        [SCALAR, at(0), at(pairs), at(2 * pairs)]
        + [at(0, 512)] * 4
        + [at(0)]
        + [whole(*item.shape) for item in more],
        out_specs,
        out,
        [pltpu.VMEM((length, 128), F32)] * 2,
        vmem=56,
    )(place, mixed, mixed, mixed, *heads, *grads, logs, *more)


def of_block(which):
    return pl.BlockSpec((1, 768, 768), lambda i: (which, 0, 0))


def rows_of(count, width):
    return pl.BlockSpec((count, width), lambda i: (i, 0))


def act_grad_kernel(place_ref, own_ref, other_ref, *refs):
    core = place_ref[0]
    out_ref, aligned_ref, held = refs[4:]
    for group in range(4):
        for ref, at in ((own_ref, core), (other_ref, 1 - core)):
            rows = pl.ds(pl.multiple_of(64 * group + 32 * at, 32), 32)
            held[rows, :] = ref[pl.ds(pl.multiple_of(64 * group + 32 * (1 - core), 32), 32), :]
    row = lax.broadcasted_iota(jnp.int32, (TILE, TILE), 0)
    col = lax.broadcasted_iota(jnp.int32, (TILE, TILE), 1)
    taken = row // 32 * 32 + row % 8 + row // 8 % 2 * 16 + row // 16 % 2 * 8
    aligned_ref[...] = nn((taken == col).astype(BF), held[...]).astype(BF)
    for i, block in enumerate(refs[:4]):
        out_ref[:, 768 * i : 768 * i + 768] = nt(aligned_ref[...], block[0]).astype(BF)


def act_grads(place, own, other, blocks):
    count = own.shape[0]
    return call(
        act_grad_kernel,
        (4,),
        [SCALAR] + [rows_of(count // 4, 768)] * 2 + [of_block(1)] * 4,
        [rows_of(count // 4, 3072), rows_of(count // 4, 768)],
        [shape(BF, count, 3072), shape(BF, count, 768)],
        [pltpu.VMEM((count // 4, 768), BF)],
        vmem=56,
    )(place, own, other, *blocks)


def expert_kernel(row_ref, grad_ref, *refs):
    act_ref, pre_ref, out_ref = refs[4:]
    rows = row_ref[...]
    total = None
    for i, block in enumerate(refs[:4]):
        cols = slice(768 * i, 768 * i + 768)
        weight = block[0]
        pre = nn(rows, weight)
        cumulative = 0.5 * (1.0 + lax.erf(pre * 0.7071067811865476))
        act_ref[:, cols] = (pre * cumulative).astype(BF)
        slope = cumulative + pre * jnp.exp(-0.5 * pre * pre) * 0.3989422804014327
        grad = (grad_ref[:, cols].astype(F32) * slope).astype(BF)
        pre_ref[:, cols] = grad
        term = nt(grad, weight)
        total = term if total is None else total + term
    out_ref[...] = total.astype(BF)


def expert(rows, act_grad, blocks):
    count = rows.shape[0]
    wide = jax.ShapeDtypeStruct((count, 3072), BF)
    return call(
        expert_kernel,
        (4,),
        [rows_of(count // 4, 768), rows_of(count // 4, 3072)] + [of_block(0)] * 4,
        [rows_of(count // 4, 3072), rows_of(count // 4, 3072), rows_of(count // 4, 768)],
        [wide, wide, jax.ShapeDtypeStruct((count, 768), BF)],
        vmem=56,
    )(rows, act_grad, *blocks)


def result_kernel(act_ref, *refs):
    terms = [nn(act_ref[:, 768 * i : 768 * i + 768], refs[i][0]) for i in range(4)]
    refs[4][...] = functools.reduce(jnp.add, terms).astype(BF)


def expert_results(activated, blocks):
    count = activated.shape[0]
    return call(
        result_kernel,
        (4,),
        [rows_of(count // 4, 3072)] + [of_block(1)] * 4,
        rows_of(count // 4, 768),
        jax.ShapeDtypeStruct((count, 768), BF),
        vmem=56,
    )(activated, *blocks)


def weight_grad_kernel(row_ref, grad_ref, act_ref, pre_ref, *refs):
    one, two = tn(row_ref[...], pre_ref[...]), tn(act_ref[...], grad_ref[...])
    if len(refs) == 1:
        refs[0][0, 0] = one.astype(BF)
        refs[0][0, 1] = two.astype(BF)
        return
    one, two = one + refs[0][0, 0].astype(F32), two + refs[0][0, 1].astype(F32)
    for step, ref in enumerate(refs[1:]):

        @pl.when(pl.program_id(0) == step)
        def _():
            ref[0] = one.astype(BF)
            ref[1] = two.astype(BF)


def weight_grads(rows, grads, activated, pre_grad, start, *others):
    count = rows.shape[0]
    whole = pl.BlockSpec((count, 768), lambda i: (0, 0))
    block = pl.BlockSpec((count, 768), lambda i: (0, i + start))
    both = pl.BlockSpec((1, 2, 768, 768), lambda i: (i, 0, 0, 0))
    single = pl.BlockSpec((2, 768, 768), lambda i: (0, 0, 0))
    return call(
        weight_grad_kernel,
        (2,),
        [whole, whole, block, block] + [both] * len(others),
        [single, single] if others else both,
        [shape(BF, 2, 768, 768)] * 2 if others else shape(BF, 2, 2, 768, 768),
        vmem=56,
    )(rows, grads, activated, pre_grad, *others)


def place_kernel(even_ref, a_ref, b_ref, in_ref, out_ref):
    from_a = (pl.program_id(1) == 0) == (even_ref[0] == 1)

    @pl.when(from_a)
    def _():
        in_ref[0] = a_ref[0].astype(F32)
        out_ref[0] = a_ref[1].astype(F32)

    @pl.when(jnp.logical_not(from_a))
    def _():
        in_ref[0] = b_ref[0].astype(F32)
        out_ref[0] = b_ref[1].astype(F32)


def place_expert_grads(even, grad_a, grad_b):
    taken = pl.BlockSpec((2, 256, 768), lambda i, e: (0, i, 0))
    given = pl.BlockSpec((1, 256, 768), lambda i, e: (e, i, 0))
    return call(
        place_kernel,
        (3, 2),
        [pl.BlockSpec(memory_space=pltpu.SMEM), taken, taken],
        [given, given],
        [jax.ShapeDtypeStruct((2, 768, 768), F32)] * 2,
    )(even.astype(jnp.int32).reshape(1), grad_a, grad_b)


def slots_of(ids):
    blocks = ids.reshape(2, 256)
    same = blocks[:, :, None] == blocks[:, None, :]
    places = jnp.arange(256, dtype=jnp.int32)
    rank = jnp.sum((same & (places[None, :] < places[:, None])).astype(jnp.int32), -1)
    slots = blocks * (2 * SLOT) + jnp.arange(2, dtype=jnp.int32)[:, None] * SLOT + rank
    return slots.reshape(512)


def slot_rows(rows, slots):
    matrix = jnp.arange(1024, dtype=jnp.int32)[:, None] == slots[None, :]
    return nn(matrix.astype(BF), rows).astype(BF)


def token_rows(rows, slots):
    matrix = slots[:, None] == jnp.arange(1024, dtype=jnp.int32)[None, :]
    return nn(matrix.astype(BF), rows)


def exchange(rows):
    return lax.all_to_all(rows.reshape(64, 16, -1), CHIPS, 0, 0, tiled=True).reshape(1024, -1)


def halve_kernel(qkv_ref, out_ref, vector_ref, halves_ref):
    row = lax.broadcasted_iota(jnp.int32, (4, 128), 0)
    col = lax.broadcasted_iota(jnp.int32, (4, 128), 1)
    columns = tn(vector_ref[...], (row == col).astype(BF)).astype(BF)
    for core in range(2):
        cuts = [qkv_ref[:, 768 * i + 384 * core : 768 * i + 384 * core + 384] for i in range(3)]
        half = jnp.concatenate(cuts + [out_ref[:, 384 * core : 384 * core + 384], columns], 1)
        for chip in range(4):
            halves_ref[4 * core + chip] = half


def gather_group(qkv, out, vectors):
    sent = call(halve_kernel, (), [WHOLE] * 3, WHOLE, shape(BF, 8, 6, 1664))(qkv, out, jnp.stack(vectors))
    return lax.all_to_all(sent, GROUP, 0, 0, tiled=True).reshape(1, 48, 1664)


def reduce_plane(grads):
    got = lax.all_to_all(grads.reshape(16, 48, -1), PLANE, 0, 0, tiled=True)
    return jnp.sum(got.astype(F32), 0)


def reduce_projections(rows, first):
    rows = rows.reshape(2, 4, 6, 1664)
    place = lax.axis_index("y")

    def part(of):
        return lax.dynamic_slice_in_dim(rows, of % 4, 1, 1).reshape(2, 6, 1664)

    total = part(place)
    for shift in (2, 1, 3):
        total = total + lax.ppermute(part(place + shift), "y", [(i, (i + shift) % 4) for i in range(4)])
    keep, give = ordered(first, total[0], total[1])
    both = ordered(first, keep, swap(give))
    qkv = jnp.stack([half[:, :1152].reshape(6, 3, 384) for half in both], 2).reshape(6, 2304)
    out = jnp.concatenate([half[:, 1152:1536] for half in both], 1)
    return qkv, out, both[0][:, 1536:1540] + both[1][:, 1536:1540]


def local(
    tokens,
    buckets,
    qkv_weight,
    output_weight,
    attend_gain,
    attend_bias,
    expert_gain,
    expert_bias,
    expert_in,
    expert_out,
    cotangent,
):
    even = lax.axis_index("y") % 2 == 0
    first = lax.axis_index("core") == 0
    place = jnp.stack((lax.axis_index("core"), lax.axis_index("y") % 2)).astype(jnp.int32)

    def halves(value, extent, axis=0):
        return ordered(
            first,
            lax.slice_in_dim(value, 0, extent, axis=axis),
            lax.slice_in_dim(value, extent, 2 * extent, axis=axis),
        )

    rows = gather_group(qkv_weight, output_weight, (attend_gain, attend_bias, expert_gain, expert_bias))
    packed = jnp.pad(buckets.astype(BF), ((0, 0), (0, 0), (0, 127)))
    packed = jnp.concatenate((tokens, packed), -1)
    packed = ordered(even, packed[0], packed[1])
    experts = jnp.stack((expert_in, expert_out), 1)
    experts = ordered(even, experts[0], experts[1])
    rows, *moving = together(rows, *packed, *experts)
    pieces = to_sequence(moving[:2])
    block_a, block_b = to_sequence(moving[2:])
    sent = jnp.broadcast_to(rows, (16, 48, 1664))
    projections = lax.all_to_all(sent, PLANE, 0, 0, tiled=True).reshape(768, 1664)

    grad_slots = slot_rows(cotangent.reshape(512, 768), slots_of(buckets.reshape(512)))
    slots = jnp.concatenate(ordered(even, pieces[0][:, 768], pieces[1][:, 768]))
    slots = slots_of(slots.astype(jnp.int32))
    others = [swap(piece) for piece in pieces]
    grad_slots, *others = together(grad_slots, *others)
    grad_rows = exchange(grad_slots)

    normed, mixed, vectors, out_mine, token_half = project(place, pieces, others, projections)
    out_theirs = swap(out_mine)
    *heads, logs = attend_forward(place, mixed)
    middle, attended, sent = leave(
        place, heads[0], swap(heads[1]), out_mine, out_theirs, token_half, vectors, slots
    )
    sent, block_a, block_b, grad_rows = together(sent, block_a, block_b, grad_rows)
    blocks = (block_a, block_b, swap(block_a), swap(block_b))
    rows = exchange(sent)
    act_grad, grad_rows = act_grads(place, grad_rows, swap(grad_rows), blocks)
    act_grad, *upstream = together(act_grad, *ordered(even, cotangent[0], cotangent[1]))
    upstream = to_sequence(upstream)
    activated, pre_grad, row_grad = expert(rows, act_grad, blocks)
    row_grad, *upstream = together(row_grad, *upstream)
    back_rows = exchange(row_grad)
    result = expert_results(activated, blocks)
    result, pre_grad = together(result, pre_grad)
    made = (rows, grad_rows, activated, pre_grad)
    theirs = weight_grads(*made, 2)
    back_rows, theirs, result = together(back_rows, theirs, result)
    result_rows = exchange(result)
    grad_a, grad_b = weight_grads(*made, 0, swap(theirs))
    back_rows, grad_a, grad_b = together(back_rows, grad_a, grad_b)
    grad_a, grad_b = lax.ppermute(grad_a, GROUP, EVEN_BACK), lax.ppermute(grad_b, GROUP, ODD_BACK)

    middle_grad, branch_grad, keep, give, sums = enter(
        place, back_rows, middle, upstream, out_mine, out_theirs, vectors, slots
    )
    keep, got, result_rows = together(keep, swap(give), result_rows)
    (early_grad,) = attend_backward(place, mixed, heads, (keep, got), logs, 0, 1)
    out_keep, out_give = halves(tn(attended, branch_grad), 384, 1)
    early = early_share(normed, early_grad, out_keep, swap(out_give.astype(BF)))
    early, mixed = together(early, mixed)
    early = reduce_plane(early)
    late_grad, keep, give = attend_backward(
        place, mixed, heads, (keep, got), logs, 1, 2, projections, early_grad
    )
    token_grad, late = finish(keep, swap(give), token_half, middle_grad, vectors, sums, normed, late_grad)
    late, grad_a, grad_b = together(late, grad_a, grad_b)
    token_grad = scatter_sequence(token_grad, even)
    block_out = scatter_sequence((middle + token_rows(result_rows, slots)).astype(BF), even)
    expert_in_grad, expert_out_grad = place_expert_grads(even, grad_a, grad_b)
    late = reduce_plane(late)
    cuts = []
    for i in range(3):
        cuts += [early[:, 128 * i : 128 * i + 128], late[:, 256 * i : 256 * i + 256]]
    summed = jnp.concatenate(cuts + [early[:, 384:], late[:, 768:]], 1)
    summed, expert_in_grad, expert_out_grad = together(summed, expert_in_grad, expert_out_grad)
    qkv_grad, outproj_grad, shares = reduce_projections(summed, first)
    return (
        block_out,
        token_grad,
        qkv_grad,
        outproj_grad,
        shares[:, 0],
        shares[:, 1],
        shares[:, 2],
        shares[:, 3],
        expert_in_grad,
        expert_out_grad,
    )


def solution(mesh):
    fine = Mesh(mesh.devices.reshape(4, 4, 2, 4), ("z", "x", "core", "y"))
    dp, every = ("z", "x", "core"), ("z", "x", "core", "y")
    rows = P(dp, "y", None)
    in_specs = (
        rows,
        rows,
        P(every, None),
        P(every, None),
        P(every),
        P(every),
        P(every),
        P(every),
        P(dp, None, "y"),
        P(dp, "y", None),
        rows,
    )
    out_specs = (
        rows,
        rows,
        P(every, None),
        P(every, None),
        P(every),
        P(every),
        P(every),
        P(every),
        P(dp, None, "y"),
        P(dp, "y", None),
    )
    return jax.shard_map(local, mesh=fine, in_specs=in_specs, out_specs=out_specs, check_vma=False)
```

```python
import functools

import jax
import jax.numpy as jnp
from jax import lax
from jax.experimental import pallas as pl
from jax.experimental.pallas import tpu as pltpu
from jax.sharding import Mesh
from jax.sharding import PartitionSpec as P

HEAD_DIM = 64
SLOT = 8
TILE = 256
EPSILON = 1e-05
MASKED = -1e30
BF = jnp.bfloat16
F32 = jnp.float32

GROUP = ("core", "y")
CHIPS = ("z", "x", "y")
PLANE = ("z", "x")
EVEN = [(k * 4 + y, (1 - y // 2) * 4 + 2 * k + y % 2) for k in range(2) for y in range(4)]
ODD = [(k * 4 + y, (1 - y // 2) * 4 + 2 * k + 1 - y % 2) for k in range(2) for y in range(4)]
EVEN_BACK = [(b, a) for a, b in EVEN]
ODD_BACK = [(b, a) for a, b in ODD]


def dot(a, b, dims):
    return lax.dot_general(a, b, (dims, ((), ())), preferred_element_type=F32)


def nn(a, b):
    return dot(a, b, ((1,), (0,)))


def nt(a, b):
    return dot(a, b, ((1,), (1,)))


def tn(a, b):
    return dot(a, b, ((0,), (0,)))


def swap(value):
    return lax.ppermute(value, "core", [(0, 1), (1, 0)])


def ordered(first, one, two):
    return jnp.where(first, one, two), jnp.where(first, two, one)


def to_sequence(pair):
    return lax.ppermute(pair[0], GROUP, EVEN), lax.ppermute(pair[1], GROUP, ODD)


def scatter_sequence(half, even):
    low, high = half[:256], half[256:]
    mine, other = ordered(even, low, high)
    mine, other = lax.ppermute(mine, GROUP, EVEN_BACK), lax.ppermute(other, GROUP, ODD_BACK)
    return jnp.stack(ordered(even, mine, other))


def together(*values):
    return lax.optimization_barrier(values)


def standardize(values):
    centered = values - jnp.mean(values, -1, keepdims=True)
    inverse = lax.rsqrt(jnp.mean(centered * centered, -1, keepdims=True) + EPSILON)
    return centered * inverse, inverse


def norm_backward(upstream, standard, inverse, gain_vec):
    scaled = upstream * gain_vec
    return inverse * (
        scaled
        - jnp.mean(scaled, -1, keepdims=True)
        - standard * jnp.mean(scaled * standard, -1, keepdims=True)
    )


def sum_rows(values):
    return jnp.sum(values, 0, keepdims=True)


def call(kernel, grid, in_specs, out_specs, out_shape, scratch=(), vmem=28):
    return pl.pallas_call(
        kernel,
        grid=grid,
        in_specs=in_specs,
        out_specs=out_specs,
        out_shape=out_shape,
        scratch_shapes=scratch,
        compiler_params=pltpu.CompilerParams(vmem_limit_bytes=vmem * 2**20),
        cost_estimate=pl.CostEstimate(flops=100_000_000, bytes_accessed=2**16, transcendentals=0),
    )


WHOLE = pl.BlockSpec(memory_space=pltpu.VMEM)
SCALAR = pl.BlockSpec(memory_space=pltpu.SMEM)


def shape(dtype, *sizes):
    return jax.ShapeDtypeStruct(sizes, dtype)


def at_core(core, extent):
    return pl.ds(pl.multiple_of(core * extent, 128), extent)


def project_kernel(
    place_ref, own_a_ref, own_b_ref, other_a_ref, other_b_ref, weight_ref,
    normed_ref, mixed_ref, vector_ref, out_ref, token_ref,
):
    core, odd = place_ref[0], place_ref[1]
    row = lax.broadcasted_iota(jnp.int32, (8, 128), 0)
    col = lax.broadcasted_iota(jnp.int32, (8, 128), 1)
    vectors = nt((row == col).astype(BF), weight_ref[:, 1536:])
    vector_ref[...] = vectors
    out_ref[...] = weight_ref[:, 1152:1536]
    token_ref[at_core(odd, TILE), :] = own_a_ref[:, :768]
    token_ref[at_core(1 - odd, TILE), :] = own_b_ref[:, :768]
    pieces = ((1 - core, odd, own_a_ref), (1 - core, 1 - odd, own_b_ref))
    pieces += ((core, odd, other_a_ref), (core, 1 - odd, other_b_ref))
    for half, quarter, ref in pieces:
        standard, _ = standardize(ref[:, :768].astype(F32))
        normed = (standard * vectors[0:1] + vectors[1:2]).astype(BF)
        normed_ref[at_core(2 * half + quarter, TILE), :] = normed
    mixed_ref[...] = nn(normed_ref[...], weight_ref[:, :1152]).astype(BF)


def project(place, pieces, others, projections):
    return call(
        project_kernel,
        (),
        [SCALAR] + [WHOLE] * 5,
        [WHOLE] * 5,
        [
            shape(BF, 1024, 768),
            shape(BF, 1024, 1152),
            shape(F32, 8, 768),
            shape(BF, 768, 384),
            shape(BF, 512, 768),
        ],
        vmem=56,
    )(place, *pieces, *others, projections)


def leave_kernel(
    place_ref, own_ref, other_ref, mine_ref, theirs_ref, token_ref, vector_ref, slot_ref,
    middle_ref, attended_ref, sent_ref,
):
    core = place_ref[0]
    here, there = at_core(core, 384), at_core(1 - core, 384)
    attended_ref[:, here] = own_ref[...]
    attended_ref[:, there] = other_ref[...]
    middle_ref[:, here] = nn(attended_ref[...], mine_ref[...])
    middle_ref[:, there] = nn(attended_ref[...], theirs_ref[...])
    middle = token_ref[...].astype(F32) + middle_ref[...]
    middle_ref[...] = middle
    second = (standardize(middle)[0] * vector_ref[2:3, :] + vector_ref[3:4, :]).astype(BF)
    slots = lax.broadcasted_iota(jnp.int32, (1024, 512), 0) == slot_ref[...]
    sent_ref[...] = nn(slots.astype(BF), second).astype(BF)


def leave(place, own, other, mine, theirs, tokens, vectors, slots):
    return call(
        leave_kernel,
        (),
        [SCALAR] + [WHOLE] * 7,
        [WHOLE] * 3,
        [shape(F32, 512, 768), shape(BF, 512, 768), shape(BF, 1024, 768)],
    )(place, own, other, mine, theirs, tokens, vectors, slots.reshape(1, 512))


def enter_kernel(
    place_ref, back_ref, middle_ref, up_a_ref, up_b_ref, mine_ref, theirs_ref, vector_ref, slot_ref,
    grad_ref, low_ref, keep_ref, give_ref, sums_ref,
):
    core, odd = place_ref[0], place_ref[1]
    here, there = at_core(core, 384), at_core(1 - core, 384)
    grad_ref[at_core(odd, TILE), :] = up_a_ref[...].astype(F32)
    grad_ref[at_core(1 - odd, TILE), :] = up_b_ref[...].astype(F32)
    slots = lax.broadcasted_iota(jnp.int32, (1024, 512), 0) == slot_ref[...]
    second_grad = tn(slots.astype(BF), back_ref[...])
    standard, inverse = standardize(middle_ref[...])
    sums_ref[...] = jnp.zeros_like(sums_ref)
    sums_ref[2:3, :] = sum_rows(second_grad * standard)
    sums_ref[3:4, :] = sum_rows(second_grad)
    grad = grad_ref[...] + norm_backward(second_grad, standard, inverse, vector_ref[2:3, :])
    grad_ref[...] = grad
    low_ref[...] = grad.astype(BF)
    for ref, rows in ((keep_ref, here), (give_ref, there)):
        total = nt(low_ref[:, here], mine_ref[rows, :]) + nt(low_ref[:, there], theirs_ref[rows, :])
        ref[...] = total.astype(BF)


def enter(place, back_rows, middle, upstream, mine, theirs, vectors, slots):
    return call(
        enter_kernel,
        (),
        [SCALAR] + [WHOLE] * 8,
        [WHOLE] * 5,
        [
            shape(F32, 512, 768),
            shape(BF, 512, 768),
            shape(BF, 512, 384),
            shape(BF, 512, 384),
            shape(F32, 8, 768),
        ],
        vmem=56,
    )(place, back_rows, middle, *upstream, mine, theirs, vectors, slots.reshape(1, 512))


def share_kernel(normed_ref, mixed_ref, kept_ref, given_ref, share_ref):
    share_ref[:, :384] = tn(normed_ref[...], mixed_ref[...]).astype(BF)
    share_ref[:, 384:] = (kept_ref[...] + given_ref[...].astype(F32)).astype(BF)


def early_share(*values):
    return call(share_kernel, (), [WHOLE] * 4, WHOLE, shape(BF, 768, 768))(*values)


def finish_kernel(
    keep_ref, got_ref, token_ref, grad_ref, vector_ref, sums_ref, normed_ref, mixed_ref, out_ref, share_ref
):
    normed_grad = keep_ref[...] + got_ref[...].astype(F32)
    standard, inverse = standardize(token_ref[...].astype(F32))
    grad = grad_ref[...] + norm_backward(normed_grad, standard, inverse, vector_ref[0:1, :])
    out_ref[...] = grad.astype(BF)
    place = lax.broadcasted_iota(jnp.int32, (8, 768), 0)
    sums = jnp.where(place == 0, sum_rows(normed_grad * standard), sums_ref[...])
    sums = jnp.where(place == 1, sum_rows(normed_grad), sums)
    row = lax.broadcasted_iota(jnp.int32, (8, 128), 0)
    col = lax.broadcasted_iota(jnp.int32, (8, 128), 1)
    share_ref[:, 768:] = tn(sums.astype(BF), (row == col).astype(BF)).astype(BF)
    share_ref[:, :768] = tn(normed_ref[...], mixed_ref[...]).astype(BF)


def finish(*values):
    return call(
        finish_kernel,
        (),
        [WHOLE] * 8,
        [WHOLE] * 2,
        [shape(BF, 512, 768), shape(BF, 768, 896)],
    )(*values)


def head_lanes(head):
    lane = lax.broadcasted_iota(jnp.int32, (TILE, 128), 1)
    return lane < HEAD_DIM if head == 0 else lane >= HEAD_DIM


def both_heads(value):
    parts = [jnp.where(head_lanes(head), value, jnp.zeros_like(value)) for head in range(2)]
    return jnp.concatenate(parts, 0)


def side_by_side(value):
    return jnp.where(head_lanes(0), value[:TILE], value[TILE:])


def attend_forward_kernel(place_ref, q_ref, k_ref, v_ref, keep_ref, give_ref, log_ref):
    row = lax.broadcasted_iota(jnp.int32, (2 * TILE, TILE), 0)
    allowed = lax.broadcasted_iota(jnp.int32, (2 * TILE, TILE), 1) <= lax.rem(row, TILE)
    for i in range(q_ref.shape[0] // TILE):
        rows = pl.ds(i * TILE, TILE)
        queries = both_heads(q_ref[rows, :] * jnp.asarray(HEAD_DIM**-0.5, BF))
        tiles = [pl.ds(j * TILE, TILE) for j in range(i + 1)]
        scores = [nt(queries, k_ref[tile, :]) for tile in tiles]
        scores[i] = jnp.where(allowed, scores[i], MASKED)
        top = functools.reduce(jnp.maximum, [jnp.max(s, axis=1, keepdims=True) for s in scores])
        weights = [jnp.exp(s - top) for s in scores]
        total = functools.reduce(jnp.add, [jnp.sum(w, axis=1, keepdims=True) for w in weights])
        terms = [nn(w.astype(BF), v_ref[tile, :]) for w, tile in zip(weights, tiles)]
        out = side_by_side(functools.reduce(jnp.add, terms) * (1.0 / total)).astype(BF)
        within, ours = pl.ds(i % 2 * TILE, TILE), place_ref[0] == 1 - i // 2

        @pl.when(ours)
        def _():
            keep_ref[within, :] = out

        @pl.when(jnp.logical_not(ours))
        def _():
            give_ref[within, :] = out

        log_ref[rows, :] = side_by_side(jnp.broadcast_to(top + jnp.log(total), (2 * TILE, 128)))


def attend_forward(place, mixed):
    length, width = mixed.shape
    pairs = width // 384

    def at(shift, rows=length):
        return pl.BlockSpec((rows, 128), lambda p: (0, p + shift))

    return call(
        attend_forward_kernel,
        (pairs,),
        [SCALAR, at(0), at(pairs), at(2 * pairs)],
        [at(0, 512), at(0, 512), at(0)],
        [shape(BF, 512, 128 * pairs), shape(BF, 512, 128 * pairs), shape(F32, length, 128 * pairs)],
        vmem=56,
    )(place, mixed, mixed, mixed)


def attend_backward_kernel(
    place_ref, q_ref, k_ref, v_ref, own_o_ref, other_o_ref, own_g_ref, other_g_ref, log_ref, *refs
):
    *others, k_sum, v_sum = refs
    out_ref = others[0] if len(others) == 1 else others[2]

    def columns(part):
        start = part * (out_ref.shape[1] // 3) + pl.program_id(0) * 128
        return pl.ds(pl.multiple_of(start, 128), 128)

    query = lax.broadcasted_iota(jnp.int32, (TILE, 2 * TILE), 1)
    allowed = lax.broadcasted_iota(jnp.int32, (TILE, 2 * TILE), 0) <= lax.rem(query, TILE)
    k_sum[...] = jnp.zeros_like(k_sum)
    v_sum[...] = jnp.zeros_like(v_sum)
    for i in range(q_ref.shape[0] // TILE):
        rows = pl.ds(i * TILE, TILE)
        within, ours = pl.ds(i % 2 * TILE, TILE), place_ref[0] == 1 - i // 2
        up = jnp.where(ours, own_g_ref[within, :], other_g_ref[within, :])
        heads = jnp.where(ours, own_o_ref[within, :], other_o_ref[within, :])
        product = (up.astype(F32) * heads.astype(F32)).T
        logs = log_ref[rows, :].T
        queries = both_heads(q_ref[rows, :] * jnp.asarray(HEAD_DIM**-0.5, BF))
        grads = both_heads(up)
        row_dots = [jnp.sum(product[64 * head : 64 * head + 64], axis=0, keepdims=True) for head in range(2)]
        row_dots = jnp.concatenate(row_dots, 1)
        log_row = jnp.concatenate([logs[0:1], logs[64:65]], 1)
        total = None
        for j in range(i + 1):
            cols = pl.ds(j * TILE, TILE)
            scores = nt(k_ref[cols, :], queries)
            if j == i:
                scores = jnp.where(allowed, scores, MASKED)
            probs = jnp.exp(scores - log_row)
            prob_grad = nt(v_ref[cols, :], grads)
            score_grad = (probs * (prob_grad - row_dots)).astype(BF)
            v_sum[cols, :] += nn(probs.astype(BF), grads)
            k_sum[cols, :] += nn(score_grad, queries)
            term = tn(score_grad, k_ref[cols, :])
            total = term if total is None else total + term
        out_ref[rows, columns(0)] = (side_by_side(total) * HEAD_DIM**-0.5).astype(BF)
    out_ref[:, columns(1)] = k_sum[...].astype(BF)
    out_ref[:, columns(2)] = v_sum[...].astype(BF)

    if len(others) > 1:
        weight_ref, before_ref, _, keep_ref, give_ref = others

        @pl.when(pl.program_id(0) == pl.num_programs(0) - 1)
        def _():
            core = place_ref[0]
            for half, ref in ((1 - core, keep_ref), (core, give_ref)):
                rows, total = at_core(half, 512), None
                for source, first in ((before_ref, 0), (out_ref, 128)):
                    width = source.shape[1] // 3
                    for part in range(3):
                        weight = weight_ref[:, 384 * part + first : 384 * part + first + width]
                        term = nt(source[rows, width * part : width * part + width], weight)
                        total = term if total is None else total + term
                ref[...] = total.astype(ref.dtype)


def attend_backward(place, mixed, heads, grads, logs, first, count, *more):
    length, width = mixed.shape
    pairs = width // 384

    def at(shift, rows=length):
        return pl.BlockSpec((rows, 128), lambda p: (0, p + shift + first))

    def whole(*sizes):
        return pl.BlockSpec(sizes, lambda p: (0, 0))

    out, out_specs = [shape(BF, length, 384 * count)], [whole(length, 384 * count)]
    if more:
        out += [shape(F32, 512, 768), shape(BF, 512, 768)]
        out_specs += [whole(512, 768)] * 2
    return call(
        attend_backward_kernel,
        (count,),
        [SCALAR, at(0), at(pairs), at(2 * pairs)]
        + [at(0, 512)] * 4
        + [at(0)]
        + [whole(*item.shape) for item in more],
        out_specs,
        out,
        [pltpu.VMEM((length, 128), F32)] * 2,
        vmem=56,
    )(place, mixed, mixed, mixed, *heads, *grads, logs, *more)


def of_block(which):
    return pl.BlockSpec((1, 768, 768), lambda i: (which, 0, 0))


def rows_of(count, width):
    return pl.BlockSpec((count, width), lambda i: (i, 0))


def act_grad_kernel(place_ref, own_ref, other_ref, *refs):
    core = place_ref[0]
    out_ref, aligned_ref, held = refs[4:]
    for group in range(4):
        for ref, at in ((own_ref, core), (other_ref, 1 - core)):
            rows = pl.ds(pl.multiple_of(64 * group + 32 * at, 32), 32)
            held[rows, :] = ref[pl.ds(pl.multiple_of(64 * group + 32 * (1 - core), 32), 32), :]
    row = lax.broadcasted_iota(jnp.int32, (TILE, TILE), 0)
    col = lax.broadcasted_iota(jnp.int32, (TILE, TILE), 1)
    taken = row // 32 * 32 + row % 8 + row // 8 % 2 * 16 + row // 16 % 2 * 8
    aligned_ref[...] = nn((taken == col).astype(BF), held[...]).astype(BF)
    for i, block in enumerate(refs[:4]):
        out_ref[:, 768 * i : 768 * i + 768] = nt(aligned_ref[...], block[0]).astype(BF)


def act_grads(place, own, other, blocks):
    count = own.shape[0]
    return call(
        act_grad_kernel,
        (4,),
        [SCALAR] + [rows_of(count // 4, 768)] * 2 + [of_block(1)] * 4,
        [rows_of(count // 4, 3072), rows_of(count // 4, 768)],
        [shape(BF, count, 3072), shape(BF, count, 768)],
        [pltpu.VMEM((count // 4, 768), BF)],
        vmem=56,
    )(place, own, other, *blocks)


def expert_kernel(row_ref, grad_ref, *refs):
    act_ref, pre_ref, out_ref, held = refs[4:]
    rows = row_ref[...]
    for i, block in enumerate(refs[:4]):
        held[:, 768 * i : 768 * i + 768] = nn(rows, block[0])
    total = None
    for i, block in enumerate(refs[:4]):
        cols = slice(768 * i, 768 * i + 768)
        pre = held[:, cols]
        cumulative = 0.5 * (1.0 + lax.erf(pre * 0.7071067811865476))
        act_ref[:, cols] = (pre * cumulative).astype(BF)
        slope = cumulative + pre * jnp.exp(-0.5 * pre * pre) * 0.3989422804014327
        grad = (grad_ref[:, cols].astype(F32) * slope).astype(BF)
        pre_ref[:, cols] = grad
        term = nt(grad, block[0])
        total = term if total is None else total + term
    out_ref[...] = total.astype(BF)


def expert(rows, act_grad, blocks):
    count = rows.shape[0]
    wide = jax.ShapeDtypeStruct((count, 3072), BF)
    return call(
        expert_kernel,
        (4,),
        [rows_of(count // 4, 768), rows_of(count // 4, 3072)] + [of_block(0)] * 4,
        [rows_of(count // 4, 3072), rows_of(count // 4, 3072), rows_of(count // 4, 768)],
        [wide, wide, jax.ShapeDtypeStruct((count, 768), BF)],
        [pltpu.VMEM((count // 4, 3072), F32)],
        vmem=56,
    )(rows, act_grad, *blocks)


def result_kernel(act_ref, *refs):
    terms = [nn(act_ref[:, 768 * i : 768 * i + 768], refs[i][0]) for i in range(4)]
    refs[4][...] = functools.reduce(jnp.add, terms).astype(BF)


def expert_results(activated, blocks):
    count = activated.shape[0]
    return call(
        result_kernel,
        (4,),
        [rows_of(count // 4, 3072)] + [of_block(1)] * 4,
        rows_of(count // 4, 768),
        jax.ShapeDtypeStruct((count, 768), BF),
        vmem=56,
    )(activated, *blocks)


def weight_grad_kernel(row_ref, grad_ref, act_ref, pre_ref, *refs):
    one, two = tn(row_ref[...], pre_ref[...]), tn(act_ref[...], grad_ref[...])
    if len(refs) == 1:
        refs[0][0, 0] = one.astype(BF)
        refs[0][0, 1] = two.astype(BF)
        return
    one, two = one + refs[0][0, 0].astype(F32), two + refs[0][0, 1].astype(F32)
    for step, ref in enumerate(refs[1:]):

        @pl.when(pl.program_id(0) == step)
        def _():
            ref[0] = one.astype(BF)
            ref[1] = two.astype(BF)


def weight_grads(rows, grads, activated, pre_grad, start, *others):
    count = rows.shape[0]
    whole = pl.BlockSpec((count, 768), lambda i: (0, 0))
    block = pl.BlockSpec((count, 768), lambda i: (0, i + start))
    both = pl.BlockSpec((1, 2, 768, 768), lambda i: (i, 0, 0, 0))
    single = pl.BlockSpec((2, 768, 768), lambda i: (0, 0, 0))
    return call(
        weight_grad_kernel,
        (2,),
        [whole, whole, block, block] + [both] * len(others),
        [single, single] if others else both,
        [shape(BF, 2, 768, 768)] * 2 if others else shape(BF, 2, 2, 768, 768),
        vmem=56,
    )(rows, grads, activated, pre_grad, *others)


def place_kernel(even_ref, a_ref, b_ref, in_ref, out_ref):
    from_a = (pl.program_id(1) == 0) == (even_ref[0] == 1)

    @pl.when(from_a)
    def _():
        in_ref[0] = a_ref[0].astype(F32)
        out_ref[0] = a_ref[1].astype(F32)

    @pl.when(jnp.logical_not(from_a))
    def _():
        in_ref[0] = b_ref[0].astype(F32)
        out_ref[0] = b_ref[1].astype(F32)


def place_expert_grads(even, grad_a, grad_b):
    taken = pl.BlockSpec((2, 256, 768), lambda i, e: (0, i, 0))
    given = pl.BlockSpec((1, 256, 768), lambda i, e: (e, i, 0))
    return call(
        place_kernel,
        (3, 2),
        [pl.BlockSpec(memory_space=pltpu.SMEM), taken, taken],
        [given, given],
        [jax.ShapeDtypeStruct((2, 768, 768), F32)] * 2,
    )(even.astype(jnp.int32).reshape(1), grad_a, grad_b)


def slots_of(ids):
    blocks = ids.reshape(2, 256)
    same = blocks[:, :, None] == blocks[:, None, :]
    places = jnp.arange(256, dtype=jnp.int32)
    rank = jnp.sum((same & (places[None, :] < places[:, None])).astype(jnp.int32), -1)
    slots = blocks * (2 * SLOT) + jnp.arange(2, dtype=jnp.int32)[:, None] * SLOT + rank
    return slots.reshape(512)


def slot_rows(rows, slots):
    matrix = jnp.arange(1024, dtype=jnp.int32)[:, None] == slots[None, :]
    return nn(matrix.astype(BF), rows).astype(BF)


def token_rows(rows, slots):
    matrix = slots[:, None] == jnp.arange(1024, dtype=jnp.int32)[None, :]
    return nn(matrix.astype(BF), rows)


def exchange(rows):
    return lax.all_to_all(rows.reshape(64, 16, -1), CHIPS, 0, 0, tiled=True).reshape(1024, -1)


def halve_kernel(qkv_ref, out_ref, vector_ref, halves_ref):
    row = lax.broadcasted_iota(jnp.int32, (4, 128), 0)
    col = lax.broadcasted_iota(jnp.int32, (4, 128), 1)
    columns = tn(vector_ref[...], (row == col).astype(BF)).astype(BF)
    for core in range(2):
        cuts = [qkv_ref[:, 768 * i + 384 * core : 768 * i + 384 * core + 384] for i in range(3)]
        half = jnp.concatenate(cuts + [out_ref[:, 384 * core : 384 * core + 384], columns], 1)
        for chip in range(4):
            halves_ref[4 * core + chip] = half


def gather_group(qkv, out, vectors):
    sent = call(halve_kernel, (), [WHOLE] * 3, WHOLE, shape(BF, 8, 6, 1664))(qkv, out, jnp.stack(vectors))
    return lax.all_to_all(sent, GROUP, 0, 0, tiled=True).reshape(1, 48, 1664)


def reduce_plane(grads):
    got = lax.all_to_all(grads.reshape(16, 48, -1), PLANE, 0, 0, tiled=True)
    return jnp.sum(got.astype(F32), 0)


def reduce_projections(rows, first):
    rows = rows.reshape(2, 4, 6, 1664)
    place = lax.axis_index("y")

    def part(of):
        return lax.dynamic_slice_in_dim(rows, of % 4, 1, 1).reshape(2, 6, 1664)

    total = part(place)
    for shift in (2, 1, 3):
        total = total + lax.ppermute(part(place + shift), "y", [(i, (i + shift) % 4) for i in range(4)])
    keep, give = ordered(first, total[0], total[1])
    both = ordered(first, keep, swap(give))
    qkv = jnp.stack([half[:, :1152].reshape(6, 3, 384) for half in both], 2).reshape(6, 2304)
    out = jnp.concatenate([half[:, 1152:1536] for half in both], 1)
    return qkv, out, both[0][:, 1536:1540] + both[1][:, 1536:1540]


def local(
    tokens,
    buckets,
    qkv_weight,
    output_weight,
    attend_gain,
    attend_bias,
    expert_gain,
    expert_bias,
    expert_in,
    expert_out,
    cotangent,
):
    even = lax.axis_index("y") % 2 == 0
    first = lax.axis_index("core") == 0
    place = jnp.stack((lax.axis_index("core"), lax.axis_index("y") % 2)).astype(jnp.int32)

    def halves(value, extent, axis=0):
        return ordered(
            first,
            lax.slice_in_dim(value, 0, extent, axis=axis),
            lax.slice_in_dim(value, extent, 2 * extent, axis=axis),
        )

    rows = gather_group(qkv_weight, output_weight, (attend_gain, attend_bias, expert_gain, expert_bias))
    packed = jnp.pad(buckets.astype(BF), ((0, 0), (0, 0), (0, 127)))
    packed = jnp.concatenate((tokens, packed), -1)
    packed = ordered(even, packed[0], packed[1])
    experts = jnp.stack((expert_in, expert_out), 1)
    experts = ordered(even, experts[0], experts[1])
    rows, *moving = together(rows, *packed, *experts)
    pieces = to_sequence(moving[:2])
    block_a, block_b = to_sequence(moving[2:])
    sent = jnp.broadcast_to(rows, (16, 48, 1664))
    projections = lax.all_to_all(sent, PLANE, 0, 0, tiled=True).reshape(768, 1664)

    grad_slots = slot_rows(cotangent.reshape(512, 768), slots_of(buckets.reshape(512)))
    slots = jnp.concatenate(ordered(even, pieces[0][:, 768], pieces[1][:, 768]))
    slots = slots_of(slots.astype(jnp.int32))
    others = [swap(piece) for piece in pieces]
    grad_slots, *others = together(grad_slots, *others)
    grad_rows = exchange(grad_slots)

    normed, mixed, vectors, out_mine, token_half = project(place, pieces, others, projections)
    out_theirs = swap(out_mine)
    *heads, logs = attend_forward(place, mixed)
    middle, attended, sent = leave(
        place, heads[0], swap(heads[1]), out_mine, out_theirs, token_half, vectors, slots
    )
    sent, block_a, block_b, grad_rows = together(sent, block_a, block_b, grad_rows)
    blocks = (block_a, block_b, swap(block_a), swap(block_b))
    rows = exchange(sent)
    act_grad, grad_rows = act_grads(place, grad_rows, swap(grad_rows), blocks)
    act_grad, *upstream = together(act_grad, *ordered(even, cotangent[0], cotangent[1]))
    upstream = to_sequence(upstream)
    activated, pre_grad, row_grad = expert(rows, act_grad, blocks)
    row_grad, *upstream = together(row_grad, *upstream)
    back_rows = exchange(row_grad)
    result = expert_results(activated, blocks)
    result, pre_grad = together(result, pre_grad)
    made = (rows, grad_rows, activated, pre_grad)
    theirs = weight_grads(*made, 2)
    back_rows, theirs, result = together(back_rows, theirs, result)
    result_rows = exchange(result)
    grad_a, grad_b = weight_grads(*made, 0, swap(theirs))
    back_rows, grad_a, grad_b = together(back_rows, grad_a, grad_b)
    grad_a, grad_b = lax.ppermute(grad_a, GROUP, EVEN_BACK), lax.ppermute(grad_b, GROUP, ODD_BACK)

    middle_grad, branch_grad, keep, give, sums = enter(
        place, back_rows, middle, upstream, out_mine, out_theirs, vectors, slots
    )
    keep, got, result_rows = together(keep, swap(give), result_rows)
    (early_grad,) = attend_backward(place, mixed, heads, (keep, got), logs, 0, 1)
    out_keep, out_give = halves(tn(attended, branch_grad), 384, 1)
    early = early_share(normed, early_grad, out_keep, swap(out_give.astype(BF)))
    early, mixed = together(early, mixed)
    early = reduce_plane(early)
    late_grad, keep, give = attend_backward(
        place, mixed, heads, (keep, got), logs, 1, 2, projections, early_grad
    )
    token_grad, late = finish(keep, swap(give), token_half, middle_grad, vectors, sums, normed, late_grad)
    late, grad_a, grad_b = together(late, grad_a, grad_b)
    token_grad = scatter_sequence(token_grad, even)
    block_out = scatter_sequence((middle + token_rows(result_rows, slots)).astype(BF), even)
    expert_in_grad, expert_out_grad = place_expert_grads(even, grad_a, grad_b)
    late = reduce_plane(late)
    cuts = []
    for i in range(3):
        cuts += [early[:, 128 * i : 128 * i + 128], late[:, 256 * i : 256 * i + 256]]
    summed = jnp.concatenate(cuts + [early[:, 384:], late[:, 768:]], 1)
    summed, expert_in_grad, expert_out_grad = together(summed, expert_in_grad, expert_out_grad)
    qkv_grad, outproj_grad, shares = reduce_projections(summed, first)
    return (
        block_out,
        token_grad,
        qkv_grad,
        outproj_grad,
        shares[:, 0],
        shares[:, 1],
        shares[:, 2],
        shares[:, 3],
        expert_in_grad,
        expert_out_grad,
    )


def solution(mesh):
    fine = Mesh(mesh.devices.reshape(4, 4, 2, 4), ("z", "x", "core", "y"))
    dp, every = ("z", "x", "core"), ("z", "x", "core", "y")
    rows = P(dp, "y", None)
    in_specs = (
        rows,
        rows,
        P(every, None),
        P(every, None),
        P(every),
        P(every),
        P(every),
        P(every),
        P(dp, None, "y"),
        P(dp, "y", None),
        rows,
    )
    out_specs = (
        rows,
        rows,
        P(every, None),
        P(every, None),
        P(every),
        P(every),
        P(every),
        P(every),
        P(dp, None, "y"),
        P(dp, "y", None),
    )
    return jax.shard_map(local, mesh=fine, in_specs=in_specs, out_specs=out_specs, check_vma=False)
```

```python
import functools

import jax
import jax.numpy as jnp
from jax import lax
from jax.experimental import pallas as pl
from jax.experimental.pallas import tpu as pltpu
from jax.sharding import Mesh
from jax.sharding import PartitionSpec as P

HEAD_DIM = 64
SLOT = 8
TILE = 256
EPSILON = 1e-05
MASKED = -1e30
BF = jnp.bfloat16
F32 = jnp.float32

GROUP = ("core", "y")
CHIPS = ("z", "x", "y")
PLANE = ("z", "x")
EVEN = [(k * 4 + y, (1 - y // 2) * 4 + 2 * k + y % 2) for k in range(2) for y in range(4)]
ODD = [(k * 4 + y, (1 - y // 2) * 4 + 2 * k + 1 - y % 2) for k in range(2) for y in range(4)]
EVEN_BACK = [(b, a) for a, b in EVEN]
ODD_BACK = [(b, a) for a, b in ODD]


def dot(a, b, dims):
    return lax.dot_general(a, b, (dims, ((), ())), preferred_element_type=F32)


def nn(a, b):
    return dot(a, b, ((1,), (0,)))


def nt(a, b):
    return dot(a, b, ((1,), (1,)))


def tn(a, b):
    return dot(a, b, ((0,), (0,)))


def swap(value):
    return lax.ppermute(value, "core", [(0, 1), (1, 0)])


def ordered(first, one, two):
    return jnp.where(first, one, two), jnp.where(first, two, one)


def to_sequence(pair):
    return lax.ppermute(pair[0], GROUP, EVEN), lax.ppermute(pair[1], GROUP, ODD)


def scatter_sequence(half, even):
    low, high = half[:256], half[256:]
    mine, other = ordered(even, low, high)
    mine, other = lax.ppermute(mine, GROUP, EVEN_BACK), lax.ppermute(other, GROUP, ODD_BACK)
    return jnp.stack(ordered(even, mine, other))


def together(*values):
    return lax.optimization_barrier(values)


def standardize(values):
    centered = values - jnp.mean(values, -1, keepdims=True)
    inverse = lax.rsqrt(jnp.mean(centered * centered, -1, keepdims=True) + EPSILON)
    return centered * inverse, inverse


def norm_backward(upstream, standard, inverse, gain_vec):
    scaled = upstream * gain_vec
    return inverse * (
        scaled
        - jnp.mean(scaled, -1, keepdims=True)
        - standard * jnp.mean(scaled * standard, -1, keepdims=True)
    )


def sum_rows(values):
    return jnp.sum(values, 0, keepdims=True)


def call(kernel, grid, in_specs, out_specs, out_shape, scratch=(), vmem=28):
    return pl.pallas_call(
        kernel,
        grid=grid,
        in_specs=in_specs,
        out_specs=out_specs,
        out_shape=out_shape,
        scratch_shapes=scratch,
        compiler_params=pltpu.CompilerParams(vmem_limit_bytes=vmem * 2**20),
        cost_estimate=pl.CostEstimate(flops=100_000_000, bytes_accessed=2**16, transcendentals=0),
    )


WHOLE = pl.BlockSpec(memory_space=pltpu.VMEM)
SCALAR = pl.BlockSpec(memory_space=pltpu.SMEM)


def shape(dtype, *sizes):
    return jax.ShapeDtypeStruct(sizes, dtype)


def at_core(core, extent):
    return pl.ds(pl.multiple_of(core * extent, 128), extent)


def project_kernel(
    place_ref, own_a_ref, own_b_ref, other_a_ref, other_b_ref, weight_ref,
    normed_ref, mixed_ref, vector_ref, out_ref, token_ref,
):
    core, odd = place_ref[0], place_ref[1]
    row = lax.broadcasted_iota(jnp.int32, (8, 128), 0)
    col = lax.broadcasted_iota(jnp.int32, (8, 128), 1)
    vectors = nt((row == col).astype(BF), weight_ref[:, 1536:])
    vector_ref[...] = vectors
    out_ref[...] = weight_ref[:, 1152:1536]
    token_ref[at_core(odd, TILE), :] = own_a_ref[:, :768]
    token_ref[at_core(1 - odd, TILE), :] = own_b_ref[:, :768]
    pieces = ((1 - core, odd, own_a_ref), (1 - core, 1 - odd, own_b_ref))
    pieces += ((core, odd, other_a_ref), (core, 1 - odd, other_b_ref))
    for half, quarter, ref in pieces:
        standard, _ = standardize(ref[:, :768].astype(F32))
        normed = (standard * vectors[0:1] + vectors[1:2]).astype(BF)
        normed_ref[at_core(2 * half + quarter, TILE), :] = normed
    mixed_ref[...] = nn(normed_ref[...], weight_ref[:, :1152]).astype(BF)


def project(place, pieces, others, projections):
    return call(
        project_kernel,
        (),
        [SCALAR] + [WHOLE] * 5,
        [WHOLE] * 5,
        [
            shape(BF, 1024, 768),
            shape(BF, 1024, 1152),
            shape(F32, 8, 768),
            shape(BF, 768, 384),
            shape(BF, 512, 768),
        ],
        vmem=56,
    )(place, *pieces, *others, projections)


def leave_kernel(
    place_ref, own_ref, other_ref, mine_ref, theirs_ref, token_ref, vector_ref, slot_ref,
    middle_ref, attended_ref, sent_ref,
):
    core = place_ref[0]
    here, there = at_core(core, 384), at_core(1 - core, 384)
    attended_ref[:, here] = own_ref[...]
    attended_ref[:, there] = other_ref[...]
    middle_ref[:, here] = nn(attended_ref[...], mine_ref[...])
    middle_ref[:, there] = nn(attended_ref[...], theirs_ref[...])
    middle = token_ref[...].astype(F32) + middle_ref[...]
    middle_ref[...] = middle
    second = (standardize(middle)[0] * vector_ref[2:3, :] + vector_ref[3:4, :]).astype(BF)
    slots = lax.broadcasted_iota(jnp.int32, (1024, 512), 0) == slot_ref[...]
    sent_ref[...] = nn(slots.astype(BF), second).astype(BF)


def leave(place, own, other, mine, theirs, tokens, vectors, slots):
    return call(
        leave_kernel,
        (),
        [SCALAR] + [WHOLE] * 7,
        [WHOLE] * 3,
        [shape(F32, 512, 768), shape(BF, 512, 768), shape(BF, 1024, 768)],
    )(place, own, other, mine, theirs, tokens, vectors, slots.reshape(1, 512))


def enter_kernel(
    place_ref, back_ref, middle_ref, up_a_ref, up_b_ref, mine_ref, theirs_ref, vector_ref, slot_ref,
    grad_ref, low_ref, keep_ref, give_ref, sums_ref,
):
    core, odd = place_ref[0], place_ref[1]
    here, there = at_core(core, 384), at_core(1 - core, 384)
    grad_ref[at_core(odd, TILE), :] = up_a_ref[...].astype(F32)
    grad_ref[at_core(1 - odd, TILE), :] = up_b_ref[...].astype(F32)
    slots = lax.broadcasted_iota(jnp.int32, (1024, 512), 0) == slot_ref[...]
    second_grad = tn(slots.astype(BF), back_ref[...])
    standard, inverse = standardize(middle_ref[...])
    sums_ref[...] = jnp.zeros_like(sums_ref)
    sums_ref[2:3, :] = sum_rows(second_grad * standard)
    sums_ref[3:4, :] = sum_rows(second_grad)
    grad = grad_ref[...] + norm_backward(second_grad, standard, inverse, vector_ref[2:3, :])
    grad_ref[...] = grad
    low_ref[...] = grad.astype(BF)
    for ref, rows in ((keep_ref, here), (give_ref, there)):
        total = nt(low_ref[:, here], mine_ref[rows, :]) + nt(low_ref[:, there], theirs_ref[rows, :])
        ref[...] = total.astype(BF)


def enter(place, back_rows, middle, upstream, mine, theirs, vectors, slots):
    return call(
        enter_kernel,
        (),
        [SCALAR] + [WHOLE] * 8,
        [WHOLE] * 5,
        [
            shape(F32, 512, 768),
            shape(BF, 512, 768),
            shape(BF, 512, 384),
            shape(BF, 512, 384),
            shape(F32, 8, 768),
        ],
        vmem=56,
    )(place, back_rows, middle, *upstream, mine, theirs, vectors, slots.reshape(1, 512))


def share_kernel(normed_ref, mixed_ref, kept_ref, given_ref, share_ref):
    share_ref[:, :384] = tn(normed_ref[...], mixed_ref[...]).astype(BF)
    share_ref[:, 384:] = (kept_ref[...] + given_ref[...].astype(F32)).astype(BF)


def early_share(*values):
    return call(share_kernel, (), [WHOLE] * 4, WHOLE, shape(BF, 768, 768))(*values)


def finish_kernel(
    keep_ref, got_ref, token_ref, grad_ref, vector_ref, sums_ref, normed_ref, mixed_ref, out_ref, share_ref
):
    normed_grad = keep_ref[...] + got_ref[...].astype(F32)
    standard, inverse = standardize(token_ref[...].astype(F32))
    grad = grad_ref[...] + norm_backward(normed_grad, standard, inverse, vector_ref[0:1, :])
    out_ref[...] = grad.astype(BF)
    place = lax.broadcasted_iota(jnp.int32, (8, 768), 0)
    sums = jnp.where(place == 0, sum_rows(normed_grad * standard), sums_ref[...])
    sums = jnp.where(place == 1, sum_rows(normed_grad), sums)
    row = lax.broadcasted_iota(jnp.int32, (8, 128), 0)
    col = lax.broadcasted_iota(jnp.int32, (8, 128), 1)
    share_ref[:, 768:] = tn(sums.astype(BF), (row == col).astype(BF)).astype(BF)
    share_ref[:, :768] = tn(normed_ref[...], mixed_ref[...]).astype(BF)


def finish(*values):
    return call(
        finish_kernel,
        (),
        [WHOLE] * 8,
        [WHOLE] * 2,
        [shape(BF, 512, 768), shape(BF, 768, 896)],
    )(*values)


def head_lanes(head):
    lane = lax.broadcasted_iota(jnp.int32, (TILE, 128), 1)
    return lane < HEAD_DIM if head == 0 else lane >= HEAD_DIM


def both_heads(value):
    parts = [jnp.where(head_lanes(head), value, jnp.zeros_like(value)) for head in range(2)]
    return jnp.concatenate(parts, 0)


def side_by_side(value):
    return jnp.where(head_lanes(0), value[:TILE], value[TILE:])


def attend_forward_kernel(place_ref, q_ref, k_ref, v_ref, keep_ref, give_ref, log_ref):
    row = lax.broadcasted_iota(jnp.int32, (2 * TILE, TILE), 0)
    allowed = lax.broadcasted_iota(jnp.int32, (2 * TILE, TILE), 1) <= lax.rem(row, TILE)
    for i in range(q_ref.shape[0] // TILE):
        rows = pl.ds(i * TILE, TILE)
        queries = both_heads(q_ref[rows, :] * jnp.asarray(HEAD_DIM**-0.5, BF))
        tiles = [pl.ds(j * TILE, TILE) for j in range(i + 1)]
        scores = [nt(queries, k_ref[tile, :]) for tile in tiles]
        scores[i] = jnp.where(allowed, scores[i], MASKED)
        top = functools.reduce(jnp.maximum, [jnp.max(s, axis=1, keepdims=True) for s in scores])
        weights = [jnp.exp(s - top) for s in scores]
        total = functools.reduce(jnp.add, [jnp.sum(w, axis=1, keepdims=True) for w in weights])
        terms = [nn(w.astype(BF), v_ref[tile, :]) for w, tile in zip(weights, tiles)]
        out = side_by_side(functools.reduce(jnp.add, terms) * (1.0 / total)).astype(BF)
        within, ours = pl.ds(i % 2 * TILE, TILE), place_ref[0] == 1 - i // 2

        @pl.when(ours)
        def _():
            keep_ref[within, :] = out

        @pl.when(jnp.logical_not(ours))
        def _():
            give_ref[within, :] = out

        log_ref[rows, :] = side_by_side(jnp.broadcast_to(top + jnp.log(total), (2 * TILE, 128)))


def attend_forward(place, mixed):
    length, width = mixed.shape
    pairs = width // 384

    def at(shift, rows=length):
        return pl.BlockSpec((rows, 128), lambda p: (0, p + shift))

    return call(
        attend_forward_kernel,
        (pairs,),
        [SCALAR, at(0), at(pairs), at(2 * pairs)],
        [at(0, 512), at(0, 512), at(0)],
        [shape(BF, 512, 128 * pairs), shape(BF, 512, 128 * pairs), shape(F32, length, 128 * pairs)],
        vmem=56,
    )(place, mixed, mixed, mixed)


def attend_backward_kernel(
    place_ref, q_ref, k_ref, v_ref, own_o_ref, other_o_ref, own_g_ref, other_g_ref, log_ref, *refs
):
    *others, k_sum, v_sum = refs
    out_ref = others[0] if len(others) == 1 else others[2]

    def columns(part):
        start = part * (out_ref.shape[1] // 3) + pl.program_id(0) * 128
        return pl.ds(pl.multiple_of(start, 128), 128)

    query = lax.broadcasted_iota(jnp.int32, (TILE, 2 * TILE), 1)
    allowed = lax.broadcasted_iota(jnp.int32, (TILE, 2 * TILE), 0) <= lax.rem(query, TILE)
    k_sum[...] = jnp.zeros_like(k_sum)
    v_sum[...] = jnp.zeros_like(v_sum)
    for i in range(q_ref.shape[0] // TILE):
        rows = pl.ds(i * TILE, TILE)
        within, ours = pl.ds(i % 2 * TILE, TILE), place_ref[0] == 1 - i // 2
        up = jnp.where(ours, own_g_ref[within, :], other_g_ref[within, :])
        heads = jnp.where(ours, own_o_ref[within, :], other_o_ref[within, :])
        product = (up.astype(F32) * heads.astype(F32)).T
        logs = log_ref[rows, :].T
        queries = both_heads(q_ref[rows, :] * jnp.asarray(HEAD_DIM**-0.5, BF))
        grads = both_heads(up)
        row_dots = [jnp.sum(product[64 * head : 64 * head + 64], axis=0, keepdims=True) for head in range(2)]
        row_dots = jnp.concatenate(row_dots, 1)
        log_row = jnp.concatenate([logs[0:1], logs[64:65]], 1)
        total = None
        for j in range(i + 1):
            cols = pl.ds(j * TILE, TILE)
            scores = nt(k_ref[cols, :], queries)
            if j == i:
                scores = jnp.where(allowed, scores, MASKED)
            probs = jnp.exp(scores - log_row)
            prob_grad = nt(v_ref[cols, :], grads)
            score_grad = (probs * (prob_grad - row_dots)).astype(BF)
            v_sum[cols, :] += nn(probs.astype(BF), grads)
            k_sum[cols, :] += nn(score_grad, queries)
            term = tn(score_grad, k_ref[cols, :])
            total = term if total is None else total + term
        out_ref[rows, columns(0)] = (side_by_side(total) * HEAD_DIM**-0.5).astype(BF)
    out_ref[:, columns(1)] = k_sum[...].astype(BF)
    out_ref[:, columns(2)] = v_sum[...].astype(BF)

    if len(others) > 1:
        weight_ref, before_ref, _, keep_ref, give_ref = others

        @pl.when(pl.program_id(0) == pl.num_programs(0) - 1)
        def _():
            core = place_ref[0]
            for half, ref in ((1 - core, keep_ref), (core, give_ref)):
                rows, total = at_core(half, 512), None
                for source, first in ((before_ref, 0), (out_ref, 128)):
                    width = source.shape[1] // 3
                    for part in range(3):
                        weight = weight_ref[:, 384 * part + first : 384 * part + first + width]
                        term = nt(source[rows, width * part : width * part + width], weight)
                        total = term if total is None else total + term
                ref[...] = total.astype(ref.dtype)


def attend_backward(place, mixed, heads, grads, logs, first, count, *more):
    length, width = mixed.shape
    pairs = width // 384

    def at(shift, rows=length):
        return pl.BlockSpec((rows, 128), lambda p: (0, p + shift + first))

    def whole(*sizes):
        return pl.BlockSpec(sizes, lambda p: (0, 0))

    out, out_specs = [shape(BF, length, 384 * count)], [whole(length, 384 * count)]
    if more:
        out += [shape(F32, 512, 768), shape(BF, 512, 768)]
        out_specs += [whole(512, 768)] * 2
    return call(
        attend_backward_kernel,
        (count,),
        [SCALAR, at(0), at(pairs), at(2 * pairs)]
        + [at(0, 512)] * 4
        + [at(0)]
        + [whole(*item.shape) for item in more],
        out_specs,
        out,
        [pltpu.VMEM((length, 128), F32)] * 2,
        vmem=56,
    )(place, mixed, mixed, mixed, *heads, *grads, logs, *more)


def of_block(which):
    return pl.BlockSpec((1, 768, 768), lambda i: (which, 0, 0))


def rows_of(count, width):
    return pl.BlockSpec((count, width), lambda i: (i, 0))


def act_grad_kernel(place_ref, own_ref, other_ref, *refs):
    core = place_ref[0]
    out_ref, aligned_ref, held = refs[4:]
    for group in range(4):
        for ref, at in ((own_ref, core), (other_ref, 1 - core)):
            rows = pl.ds(pl.multiple_of(64 * group + 32 * at, 32), 32)
            held[rows, :] = ref[pl.ds(pl.multiple_of(64 * group + 32 * (1 - core), 32), 32), :]
    row = lax.broadcasted_iota(jnp.int32, (TILE, TILE), 0)
    col = lax.broadcasted_iota(jnp.int32, (TILE, TILE), 1)
    taken = row // 32 * 32 + row % 8 + row // 8 % 2 * 16 + row // 16 % 2 * 8
    aligned_ref[...] = nn((taken == col).astype(BF), held[...]).astype(BF)
    for i, block in enumerate(refs[:4]):
        out_ref[:, 768 * i : 768 * i + 768] = nt(aligned_ref[...], block[0]).astype(BF)


def act_grads(place, own, other, blocks):
    count = own.shape[0]
    return call(
        act_grad_kernel,
        (4,),
        [SCALAR] + [rows_of(count // 4, 768)] * 2 + [of_block(1)] * 4,
        [rows_of(count // 4, 3072), rows_of(count // 4, 768)],
        [shape(BF, count, 3072), shape(BF, count, 768)],
        [pltpu.VMEM((count // 4, 768), BF)],
        vmem=56,
    )(place, own, other, *blocks)


def expert_kernel(row_ref, grad_ref, *refs):
    act_ref, pre_ref, out_ref, held = refs[4:]
    rows = row_ref[...]
    for i, block in enumerate(refs[:4]):
        held[:, 768 * i : 768 * i + 768] = nn(rows, block[0])
    total = None
    for i, block in enumerate(refs[:4]):
        cols = slice(768 * i, 768 * i + 768)
        pre = held[:, cols]
        cumulative = 0.5 * (1.0 + lax.erf(pre * 0.7071067811865476))
        act_ref[:, cols] = (pre * cumulative).astype(BF)
        slope = cumulative + pre * jnp.exp(-0.5 * pre * pre) * 0.3989422804014327
        grad = (grad_ref[:, cols].astype(F32) * slope).astype(BF)
        pre_ref[:, cols] = grad
        term = nt(grad, block[0])
        total = term if total is None else total + term
    out_ref[...] = total.astype(BF)


def expert(rows, act_grad, blocks):
    count = rows.shape[0]
    wide = jax.ShapeDtypeStruct((count, 3072), BF)
    return call(
        expert_kernel,
        (4,),
        [rows_of(count // 4, 768), rows_of(count // 4, 3072)] + [of_block(0)] * 4,
        [rows_of(count // 4, 3072), rows_of(count // 4, 3072), rows_of(count // 4, 768)],
        [wide, wide, jax.ShapeDtypeStruct((count, 768), BF)],
        [pltpu.VMEM((count // 4, 3072), F32)],
        vmem=56,
    )(rows, act_grad, *blocks)


def result_kernel(act_ref, *refs):
    terms = [nn(act_ref[:, 768 * i : 768 * i + 768], refs[i][0]) for i in range(4)]
    refs[4][...] = functools.reduce(jnp.add, terms).astype(BF)


def expert_results(activated, blocks):
    count = activated.shape[0]
    return call(
        result_kernel,
        (4,),
        [rows_of(count // 4, 3072)] + [of_block(1)] * 4,
        rows_of(count // 4, 768),
        jax.ShapeDtypeStruct((count, 768), BF),
        vmem=56,
    )(activated, *blocks)


def weight_grad_kernel(row_ref, grad_ref, act_ref, pre_ref, *refs):
    one, two = tn(row_ref[...], pre_ref[...]), tn(act_ref[...], grad_ref[...])
    if len(refs) == 1:
        refs[0][0, 0] = one.astype(BF)
        refs[0][0, 1] = two.astype(BF)
        return
    one, two = one + refs[0][0, 0].astype(F32), two + refs[0][0, 1].astype(F32)
    for step, ref in enumerate(refs[1:]):

        @pl.when(pl.program_id(0) == step)
        def _():
            ref[0] = one.astype(BF)
            ref[1] = two.astype(BF)


def weight_grads(rows, grads, activated, pre_grad, start, *others):
    count = rows.shape[0]
    whole = pl.BlockSpec((count, 768), lambda i: (0, 0))
    block = pl.BlockSpec((count, 768), lambda i: (0, i + start))
    both = pl.BlockSpec((1, 2, 768, 768), lambda i: (i, 0, 0, 0))
    single = pl.BlockSpec((2, 768, 768), lambda i: (0, 0, 0))
    return call(
        weight_grad_kernel,
        (2,),
        [whole, whole, block, block] + [both] * len(others),
        [single, single] if others else both,
        [shape(BF, 2, 768, 768)] * 2 if others else shape(BF, 2, 2, 768, 768),
        vmem=56,
    )(rows, grads, activated, pre_grad, *others)


def place_kernel(even_ref, a_ref, b_ref, in_ref, out_ref):
    from_a = (pl.program_id(1) == 0) == (even_ref[0] == 1)

    @pl.when(from_a)
    def _():
        in_ref[0] = a_ref[0].astype(F32)
        out_ref[0] = a_ref[1].astype(F32)

    @pl.when(jnp.logical_not(from_a))
    def _():
        in_ref[0] = b_ref[0].astype(F32)
        out_ref[0] = b_ref[1].astype(F32)


def place_expert_grads(even, grad_a, grad_b):
    taken = pl.BlockSpec((2, 256, 768), lambda i, e: (0, i, 0))
    given = pl.BlockSpec((1, 256, 768), lambda i, e: (e, i, 0))
    return call(
        place_kernel,
        (3, 2),
        [pl.BlockSpec(memory_space=pltpu.SMEM), taken, taken],
        [given, given],
        [jax.ShapeDtypeStruct((2, 768, 768), F32)] * 2,
    )(even.astype(jnp.int32).reshape(1), grad_a, grad_b)


def slots_of(ids):
    blocks = ids.reshape(2, 256)
    same = blocks[:, :, None] == blocks[:, None, :]
    places = jnp.arange(256, dtype=jnp.int32)
    rank = jnp.sum((same & (places[None, :] < places[:, None])).astype(jnp.int32), -1)
    slots = blocks * (2 * SLOT) + jnp.arange(2, dtype=jnp.int32)[:, None] * SLOT + rank
    return slots.reshape(512)


def slot_rows(rows, slots):
    matrix = jnp.arange(1024, dtype=jnp.int32)[:, None] == slots[None, :]
    return nn(matrix.astype(BF), rows).astype(BF)


def token_rows(rows, slots):
    matrix = slots[:, None] == jnp.arange(1024, dtype=jnp.int32)[None, :]
    return nn(matrix.astype(BF), rows)


def exchange(rows):
    return lax.all_to_all(rows.reshape(64, 16, -1), CHIPS, 0, 0, tiled=True).reshape(1024, -1)


def halve_kernel(qkv_ref, out_ref, vector_ref, halves_ref):
    row = lax.broadcasted_iota(jnp.int32, (4, 128), 0)
    col = lax.broadcasted_iota(jnp.int32, (4, 128), 1)
    columns = tn(vector_ref[...], (row == col).astype(BF)).astype(BF)
    for core in range(2):
        cuts = [qkv_ref[:, 768 * i + 384 * core : 768 * i + 384 * core + 384] for i in range(3)]
        half = jnp.concatenate(cuts + [out_ref[:, 384 * core : 384 * core + 384], columns], 1)
        for chip in range(4):
            halves_ref[4 * core + chip] = half


def gather_group(qkv, out, vectors):
    sent = call(halve_kernel, (), [WHOLE] * 3, WHOLE, shape(BF, 8, 6, 1664))(qkv, out, jnp.stack(vectors))
    return lax.all_to_all(sent, GROUP, 0, 0, tiled=True).reshape(1, 48, 1664)


def reduce_plane(grads):
    got = lax.all_to_all(grads.reshape(16, 48, -1), PLANE, 0, 0, tiled=True)
    return jnp.sum(got.astype(F32), 0)


def reduce_projections(rows, first):
    rows = rows.reshape(2, 4, 6, 1664)
    place = lax.axis_index("y")

    def part(of):
        return lax.dynamic_slice_in_dim(rows, of % 4, 1, 1).reshape(2, 6, 1664)

    total = part(place)
    for shift in (2, 1, 3):
        total = total + lax.ppermute(part(place + shift), "y", [(i, (i + shift) % 4) for i in range(4)])
    keep, give = ordered(first, total[0], total[1])
    both = ordered(first, keep, swap(give))
    qkv = jnp.stack([half[:, :1152].reshape(6, 3, 384) for half in both], 2).reshape(6, 2304)
    out = jnp.concatenate([half[:, 1152:1536] for half in both], 1)
    return qkv, out, both[0][:, 1536:1540] + both[1][:, 1536:1540]


def local(
    tokens,
    buckets,
    qkv_weight,
    output_weight,
    attend_gain,
    attend_bias,
    expert_gain,
    expert_bias,
    expert_in,
    expert_out,
    cotangent,
):
    even = lax.axis_index("y") % 2 == 0
    first = lax.axis_index("core") == 0
    place = jnp.stack((lax.axis_index("core"), lax.axis_index("y") % 2)).astype(jnp.int32)

    def halves(value, extent, axis=0):
        return ordered(
            first,
            lax.slice_in_dim(value, 0, extent, axis=axis),
            lax.slice_in_dim(value, extent, 2 * extent, axis=axis),
        )

    rows = gather_group(qkv_weight, output_weight, (attend_gain, attend_bias, expert_gain, expert_bias))
    packed = jnp.pad(buckets.astype(BF), ((0, 0), (0, 0), (0, 127)))
    packed = jnp.concatenate((tokens, packed), -1)
    packed = ordered(even, packed[0], packed[1])
    odd = lax.axis_index("y") % 2
    experts = [
        jnp.concatenate([lax.dynamic_slice_in_dim(value, which, 1, 0) for value in (expert_in, expert_out)])
        for which in (odd, 1 - odd)
    ]
    rows, *moving = together(rows, *packed, *experts)
    pieces = to_sequence(moving[:2])
    block_a, block_b = to_sequence(moving[2:])
    sent = jnp.broadcast_to(rows, (16, 48, 1664))
    projections = lax.all_to_all(sent, PLANE, 0, 0, tiled=True).reshape(768, 1664)

    grad_slots = slot_rows(cotangent.reshape(512, 768), slots_of(buckets.reshape(512)))
    slots = jnp.concatenate(ordered(even, pieces[0][:, 768], pieces[1][:, 768]))
    slots = slots_of(slots.astype(jnp.int32))
    others = [swap(piece) for piece in pieces]
    grad_slots, *others = together(grad_slots, *others)
    grad_rows = exchange(grad_slots)

    normed, mixed, vectors, out_mine, token_half = project(place, pieces, others, projections)
    out_theirs = swap(out_mine)
    *heads, logs = attend_forward(place, mixed)
    middle, attended, sent = leave(
        place, heads[0], swap(heads[1]), out_mine, out_theirs, token_half, vectors, slots
    )
    sent, block_a, block_b, grad_rows = together(sent, block_a, block_b, grad_rows)
    blocks = (block_a, block_b, swap(block_a), swap(block_b))
    rows = exchange(sent)
    act_grad, grad_rows = act_grads(place, grad_rows, swap(grad_rows), blocks)
    act_grad, *upstream = together(act_grad, *ordered(even, cotangent[0], cotangent[1]))
    upstream = to_sequence(upstream)
    activated, pre_grad, row_grad = expert(rows, act_grad, blocks)
    row_grad, *upstream = together(row_grad, *upstream)
    back_rows = exchange(row_grad)
    result = expert_results(activated, blocks)
    result, pre_grad = together(result, pre_grad)
    made = (rows, grad_rows, activated, pre_grad)
    theirs = weight_grads(*made, 2)
    back_rows, theirs, result = together(back_rows, theirs, result)
    result_rows = exchange(result)
    grad_a, grad_b = weight_grads(*made, 0, swap(theirs))
    back_rows, grad_a, grad_b = together(back_rows, grad_a, grad_b)
    grad_a, grad_b = lax.ppermute(grad_a, GROUP, EVEN_BACK), lax.ppermute(grad_b, GROUP, ODD_BACK)

    middle_grad, branch_grad, keep, give, sums = enter(
        place, back_rows, middle, upstream, out_mine, out_theirs, vectors, slots
    )
    keep, got, result_rows = together(keep, swap(give), result_rows)
    (early_grad,) = attend_backward(place, mixed, heads, (keep, got), logs, 0, 1)
    out_keep, out_give = halves(tn(attended, branch_grad), 384, 1)
    early = early_share(normed, early_grad, out_keep, swap(out_give.astype(BF)))
    early, mixed = together(early, mixed)
    early = reduce_plane(early)
    late_grad, keep, give = attend_backward(
        place, mixed, heads, (keep, got), logs, 1, 2, projections, early_grad
    )
    token_grad, late = finish(keep, swap(give), token_half, middle_grad, vectors, sums, normed, late_grad)
    late, grad_a, grad_b = together(late, grad_a, grad_b)
    token_grad = scatter_sequence(token_grad, even)
    block_out = scatter_sequence((middle + token_rows(result_rows, slots)).astype(BF), even)
    expert_in_grad, expert_out_grad = place_expert_grads(even, grad_a, grad_b)
    late = reduce_plane(late)
    cuts = []
    for i in range(3):
        cuts += [early[:, 128 * i : 128 * i + 128], late[:, 256 * i : 256 * i + 256]]
    summed = jnp.concatenate(cuts + [early[:, 384:], late[:, 768:]], 1)
    summed, expert_in_grad, expert_out_grad = together(summed, expert_in_grad, expert_out_grad)
    qkv_grad, outproj_grad, shares = reduce_projections(summed, first)
    return (
        block_out,
        token_grad,
        qkv_grad,
        outproj_grad,
        shares[:, 0],
        shares[:, 1],
        shares[:, 2],
        shares[:, 3],
        expert_in_grad,
        expert_out_grad,
    )


def solution(mesh):
    fine = Mesh(mesh.devices.reshape(4, 4, 2, 4), ("z", "x", "core", "y"))
    dp, every = ("z", "x", "core"), ("z", "x", "core", "y")
    rows = P(dp, "y", None)
    in_specs = (
        rows,
        rows,
        P(every, None),
        P(every, None),
        P(every),
        P(every),
        P(every),
        P(every),
        P(dp, None, "y"),
        P(dp, "y", None),
        rows,
    )
    out_specs = (
        rows,
        rows,
        P(every, None),
        P(every, None),
        P(every),
        P(every),
        P(every),
        P(every),
        P(dp, None, "y"),
        P(dp, "y", None),
    )
    return jax.shard_map(local, mesh=fine, in_specs=in_specs, out_specs=out_specs, check_vma=False)
```
